32 devices in a mesh: seq: 16 (over z, x, core), ch: 2 (over y).
Axes of the slice: x: 2, y: 2, z: 4, core: 2. Of those that a mesh axis runs over, the one named last changes fastest.
Arguments:
- q_proj: bfloat16 [4096, 8192], P('seq', 'ch'), may hold values from -60 to 60
- k_proj: bfloat16 [4096, 8192], P('seq', 'ch'), may hold values from -6 to 6
- v_proj: bfloat16 [4096, 8192], P('seq', 'ch'), may hold values from -6 to 6
- short_filter: float32 [9, 8192], P(None, 'ch'), may hold values from -3 to 3
- log_decay: float32 [512, 16], P('ch'), may hold values from -0.1 to -0.00012207031
- residue: float32 [512, 16], P('ch'), may hold values from -15 to 15
- skip_bias: float32 [8192], P('ch'), may hold values from -4 to 4
- norm_gain: float32 [8192], P('ch'), may hold values from 0.25 to 1.75
Outputs:
- mixed_out: bfloat16 [4096, 8192], P('seq', 'ch')
The draws below stay inside these ranges and needn't reach their ends.
All inputs are finite; a program needn't handle non-finite values.
Results may differ from the reference program's by a relative error of at most 0.0058.
Values may be sent and summed in bfloat16 or wider, within the bound.
A program may use at most 128 MiB of HBM per device.

```python
import math
import jax
import jax.numpy as jnp
from jax import lax

D = 8192
GROUP = 16
MODES = 16
TOK_DEV = 256
LENGTH = 4096
GROUPS = 512


def draw_q_proj(key, part):
    key_one, key_two = jax.random.split(key)
    values = jnp.clip(jax.random.normal(key_one, (LENGTH, D), jnp.float32), -6.0, 6.0)
    row_scale = jnp.exp(math.log(10.0) * jax.random.uniform(key_two, (LENGTH, 1), jnp.float32))
    return (values * row_scale).astype(jnp.bfloat16)


def draw_log_decay(key, part):
    key_one, key_two, key_three, key_four = jax.random.split(key, 4)
    slow_rate = jnp.exp(jax.random.uniform(key_one, (GROUPS, MODES), jnp.float32, math.log(0.5), math.log(2.0))) / LENGTH
    middle_rate = jnp.exp(jax.random.uniform(key_two, (GROUPS, MODES), jnp.float32, math.log(0.3), math.log(4.0))) / TOK_DEV
    middle_rate = jnp.minimum(middle_rate, 0.1)
    fast_rate = jnp.exp(jax.random.uniform(key_three, (GROUPS, MODES), jnp.float32, math.log(0.02), math.log(0.1)))
    share_slow = 0.4
    share_middle = 0.35
    picker = jax.random.uniform(key_four, (GROUPS, MODES), jnp.float32)
    is_slow = picker < share_slow
    is_middle = jnp.logical_and(picker >= share_slow, picker < share_slow + share_middle)
    rate = jnp.where(is_slow, slow_rate, jnp.where(is_middle, middle_rate, fast_rate))
    return -rate


def draw_residue(key, part):
    values = jnp.clip(jax.random.normal(key, (GROUPS, MODES), jnp.float32), -6.0, 6.0)
    group_scale = 0.25 * jnp.exp(math.log(10.0) * jnp.arange(GROUPS, dtype=jnp.float32) / GROUPS)
    return values * group_scale[:, None]


def levels(rng, extent, pieces, least, high):
    level = 1.0
    for position, blocks in pieces:
        steps = jax.random.uniform(jax.random.fold_in(jax.random.fold_in(rng, 6), position), (blocks,), jnp.float32, least / len(pieces), high / len(pieces))
        level = level * jnp.repeat(jnp.exp(steps), extent[position] // blocks).reshape((-1,) + (1,) * (len(extent) - 1 - position))
    return level


def gaussian(stream_key, extent, scale, most, shards=(), kind=jnp.bfloat16):
    values = jax.random.normal(stream_key, extent, jnp.float32) * scale
    if len(shards) > 0:
        values = levels(stream_key, extent, shards, -0.22, 0.18) * values
    return jnp.clip(values, min=-most, max=most).astype(kind)


def setup_inputs(seed: int = 0) -> dict:
    key_list = jax.random.split(jax.random.key(seed), 9)
    q_proj = draw_q_proj(jax.random.fold_in(key_list[8], 71), 0)
    k_proj = gaussian(key_list[1], (LENGTH, D), 1.0, 6.0, ((0, 16), (1, 2)))
    v_proj = gaussian(key_list[2], (LENGTH, D), 1.0, 6.0, ((0, 16), (1, 2)))
    short_filter = gaussian(key_list[3], (9, D), 0.5, 3.0, ((1, 2),), jnp.float32)
    log_decay = draw_log_decay(jax.random.fold_in(key_list[8], 71), 0)
    residue = draw_residue(jax.random.fold_in(key_list[8], 71), 0)
    skip_bias = gaussian(key_list[6], (D,), 1.0, 4.0, ((0, 2),), jnp.float32)
    norm_gain = jnp.clip(1.0 + 0.15 * jax.random.normal(key_list[7], (D,), jnp.float32), 0.25, 1.75)
    return dict(q_proj=q_proj, k_proj=k_proj, v_proj=v_proj, short_filter=short_filter, log_decay=log_decay, residue=residue, skip_bias=skip_bias, norm_gain=norm_gain)


def short_conv(current, earlier, taps):
    padded = jnp.concatenate([earlier, current], axis=0)
    return taps[0] * padded[2:] + taps[1] * padded[1:-1] + taps[2] * padded[:-2]

def block_toeplitz(log_decay, weight, block):
    groups, modes = log_decay.shape
    offsets = (jnp.arange(block)[:, None] - jnp.arange(block)[None, :]).astype(jnp.float32)
    causal = offsets >= 0.0
    lagged = jnp.maximum(offsets, 0.0)
    toeplitz = jnp.zeros((groups, block, block), jnp.float32)
    for mode_index in range(modes):
        rate = log_decay[:, mode_index][:, None, None]
        toeplitz = toeplitz + weight[:, mode_index][:, None, None] * jnp.exp(lagged[None] * rate)
    return jnp.where(causal[None], toeplitz, jnp.float32(0.0))

def local_filter(mixed_in, log_decay, weight, size_group):
    tok_rows, channels = mixed_in.shape
    groups, modes = log_decay.shape
    block = min(128, tok_rows)
    count = tok_rows // block
    highest = lax.Precision.HIGHEST
    lag = jnp.arange(block, dtype=jnp.float32)
    toeplitz = block_toeplitz(log_decay, weight, block)
    entering = jnp.exp((lag + 1.0)[None, :, None] * log_decay[:, None, :]) * weight[:, None, :]
    leaving = jnp.exp((block - 1.0 - lag)[None, :, None] * log_decay[:, None, :])
    block_decay = jnp.exp(block * log_decay)
    blocks = mixed_in.reshape(count, block, groups, size_group)

    def advance(state, inputs_block):
        values = inputs_block.astype(jnp.float32)
        local_part = jnp.einsum('gab,bgk->agk', toeplitz, values, precision=highest)
        carried = jnp.einsum('gam,gkm->agk', entering, state, precision=highest)
        new_state = state * block_decay[:, None, :] + jnp.einsum('gbm,bgk->gkm', leaving, values, precision=highest)
        return (new_state, local_part + carried)
    start_state = jnp.zeros((groups, size_group, modes), jnp.float32)
    final_state, outputs = lax.scan(advance, start_state, blocks)
    return (outputs.reshape(tok_rows, channels), final_state)

def reference(q_proj, k_proj, v_proj, short_filter, log_decay, residue, skip_bias, norm_gain):
    zero_rows = jnp.zeros((2, D), jnp.float32)
    q_short = short_conv(q_proj.astype(jnp.float32), zero_rows, short_filter[0:3]).astype(jnp.bfloat16)
    q_short = lax.optimization_barrier(q_short)
    k_short = short_conv(k_proj.astype(jnp.float32), zero_rows, short_filter[3:6])
    v_short = short_conv(v_proj.astype(jnp.float32), zero_rows, short_filter[6:9])
    mixed_in = (k_short * v_short).astype(jnp.bfloat16)
    mixed_in = lax.optimization_barrier(mixed_in)
    pole = jnp.exp(log_decay)
    weight = residue * jnp.sqrt(1.0 - pole * pole)
    conv_out, final_state = local_filter(mixed_in, log_decay, weight, GROUP)
    filtered = conv_out + skip_bias * mixed_in.astype(jnp.float32)
    gated = q_short.astype(jnp.float32) * filtered
    mean_square = lax.optimization_barrier(jnp.mean(gated * gated, axis=1, keepdims=True))
    return (gated * lax.rsqrt(mean_square + 1e-05) * norm_gain).astype(jnp.bfloat16)
```

```python
import functools
import jax
import jax.numpy as jnp
from jax import lax
from jax.experimental import pallas as pl
from jax.experimental.pallas import tpu as pltpu
from jax.sharding import PartitionSpec as P

LANES = 128
MESH = pl.DeviceIdType.MESH
f32 = jnp.float32
bf16 = jnp.bfloat16


def tile_at(i):
    return pl.ds(pl.multiple_of(i * LANES, LANES), LANES)


def kernel(n, nch, rounds, modes, q_hbm, k_hbm, v_hbm, taps_hbm, decay_hbm, residue_hbm, skip_hbm, gain_hbm,
           out_ref, q_ref, k_ref, v_ref, taps_ref, decay_flat, residue_flat, skip_ref, gain_ref,
           tails, decay_ref, residue_ref, halo_out, halo_in, pad, leaving, hrev, entering, mixed, conv, rate, wide_weight,
           total, carry, carry_in, first_out, first_in, state_out, state_in, square, square_out, square_in,
           halo_send, halo_recv, state_send, state_recv, square_send, square_recv, load_sem, tail_sem, carry_send, carry_recv):
    tok, channels = q_ref.shape
    half = tok // 2
    tiles = channels // LANES
    per = LANES // modes
    me = lax.axis_index("seq")
    mych = lax.axis_index("ch")
    right, left = lax.rem(me + 1, n), lax.rem(me + n - 1, n)

    def partner(bit):
        return me + bit * (1 - 2 * lax.rem(lax.div(me, bit), 2))

    def scan_copy(r):
        return pltpu.make_async_remote_copy(
            state_out.at[r] if r else first_out, state_in.at[r] if r else first_in, state_send.at[r], state_recv.at[r],
            device_id={"seq": partner(1 << r)}, device_id_type=MESH)

    order = ((decay_hbm, decay_flat), (residue_hbm, residue_flat), (k_hbm, k_ref), (v_hbm, v_ref), (taps_hbm, taps_ref),
             (skip_hbm, skip_ref), (q_hbm, q_ref), (gain_hbm, gain_ref))
    tail_loads = [pltpu.make_async_copy(ref.at[tok - 16:tok, :], tails.at[j], tail_sem.at[j])
                  for j, ref in enumerate((q_hbm, k_hbm, v_hbm))]
    loads = [pltpu.make_async_copy(src, dst, load_sem.at[j]) for j, (src, dst) in enumerate(order)]
    for load in tail_loads + loads:
        load.start()
    barrier = pltpu.get_barrier_semaphore()
    for other in [right, left] + [partner(1 << r) for r in range(rounds)]:
        pl.semaphore_signal(barrier, inc=1, device_id={"seq": other}, device_id_type=MESH)
    for d in range(1, nch):
        pl.semaphore_signal(barrier, inc=1, device_id={"ch": lax.rem(mych + d, nch)}, device_id_type=MESH)

    halo_out[...] = jnp.zeros_like(halo_out)
    for j in range(3):
        tail_loads[j].wait()
        halo_out[2 * j:2 * j + 2, :] = tails[j].astype(f32)[14:16]
    pl.semaphore_wait(barrier, 2 + rounds + nch - 1)

    halo = pltpu.make_async_remote_copy(halo_out, halo_in, halo_send, halo_recv,
                                        device_id={"seq": right}, device_id_type=MESH)

    @pl.when(me < n - 1)
    def _():
        halo.start()

    lane = lax.broadcasted_iota(jnp.int32, (1, LANES), 1)
    lane_group = lane // modes
    lags_rev = (tok - 1 - lax.broadcasted_iota(jnp.int32, (1, tok), 1)).astype(f32)

    spread = (lax.broadcasted_iota(jnp.int32, (modes, LANES), 1) % modes
              == lax.broadcasted_iota(jnp.int32, (modes, LANES), 0)).astype(f32)
    after = (lax.broadcasted_iota(jnp.int32, (tok, 1), 0) + 1).astype(f32)
    sub = lax.broadcasted_iota(jnp.int32, (per, LANES), 0)
    sub_lane = lax.broadcasted_iota(jnp.int32, (per, LANES), 1) // modes

    def prepare(i, _):
        logs = decay_ref[pl.ds(pl.multiple_of(i * per, per), per), :]
        res = residue_ref[pl.ds(pl.multiple_of(i * per, per), per), :]
        pole = jnp.exp(logs)
        weight = res * jnp.sqrt(1.0 - pole * pole)
        cols, wcols = logs.T, weight.T
        rows = []
        wide_rate = jnp.zeros((modes, LANES), f32)
        wide_w = jnp.zeros((modes, LANES), f32)
        for j in range(per):
            col, wcol = cols[:, j:j + 1], wcols[:, j:j + 1]
            power = jnp.exp(col * lags_rev)
            leaving[pl.ds(pl.multiple_of(i * LANES, LANES) + j * modes, modes), :] = power.astype(bf16)
            rows.append(jnp.sum(power * wcol, axis=0, keepdims=True))
            wide_rate = jnp.where(lane_group == j, col, wide_rate)
            wide_w = jnp.where(lane_group == j, wcol, wide_w)
        hrev[pl.ds(pl.multiple_of(i * per, per), per), :] = jnp.concatenate(rows, axis=0)
        rate[:, tile_at(i)] = wide_rate
        wide_weight[:, tile_at(i)] = wide_w
        return 0

    loads[0].wait()
    loads[1].wait()
    decay_ref[...] = decay_flat[...].T
    residue_ref[...] = residue_flat[...].T
    lax.fori_loop(0, tiles, prepare, 0)
    for load in loads[2:6]:
        load.wait()

    @pl.when(me > 0)
    def _():
        halo.wait_recv()

    @pl.when(me == 0)
    def _():
        halo_in[...] = jnp.zeros_like(halo_in)

    def short(ref, which, i, slot=0):
        place = 3 * slot + which
        pad[place, 8:8 + tok, :] = ref[:, tile_at(i)].astype(f32)
        pad[place, 0:8, :] = jnp.concatenate(
            [jnp.zeros((6, LANES), f32), halo_in[2 * which:2 * which + 2, tile_at(i)]], axis=0)
        a = [taps_ref[3 * which + t:3 * which + t + 1, tile_at(i)] for t in range(3)]
        return a[0] * pad[place, 8:8 + tok, :] + a[1] * pad[place, 7:7 + tok, :] + a[2] * pad[place, 6:6 + tok, :]

    def summarize(i, _):
        pair = [2 * i, 2 * i + 1]
        values = [(short(k_ref, 1, t, u) * short(v_ref, 2, t, u)).astype(bf16) for u, t in enumerate(pair)]
        spreadout = [jnp.dot(leaving[tile_at(t), :], values[u], preferred_element_type=f32) for u, t in enumerate(pair)]
        for u, t in enumerate(pair):
            state = jnp.zeros((modes, LANES), f32)
            for j in range(per):
                state = jnp.where(lane_group == j, spreadout[u][j * modes:(j + 1) * modes], state)
            mixed[:, tile_at(t)] = values[u]
            total[:, tile_at(t)] = state
            first_out[:, tile_at(t)] = state.astype(bf16)
        return 0

    lax.fori_loop(0, tiles // 2, summarize, 0)

    causal = (lax.broadcasted_iota(jnp.int32, (half, tok), 1)
              <= lax.broadcasted_iota(jnp.int32, (half, tok), 0) + half)

    def convolve(i, _):
        values = mixed[:, tile_at(i)]
        first, second = values[:half], values[half:]
        right_side = jnp.concatenate(
            [jnp.concatenate([jnp.zeros_like(first), first], axis=1),
             jnp.concatenate([first, second], axis=1)], axis=0)
        lines = hrev[pl.ds(pl.multiple_of(i * per, per), per), :]
        blocks = []
        for j in range(per):
            line = jnp.broadcast_to(lines[j:j + 1], (half, tok))
            block = pltpu.roll(line, half + 1, 1, stride=1, stride_axis=0)
            blocks.append(jnp.where(causal, block, 0.0).astype(bf16))
        product = jnp.dot(jnp.concatenate(blocks, axis=0), right_side, preferred_element_type=f32)
        low = jnp.zeros((half, LANES), f32)
        high = jnp.zeros((half, LANES), f32)
        for j in range(per):
            part = product[j * half:(j + 1) * half]
            low = jnp.where(lane_group == j, part[:, :LANES], low)
            high = jnp.where(lane_group == j, part[:, LANES:], high)
        skip = skip_ref[:, tile_at(i)]
        conv[:half, tile_at(i)] = low + skip * first.astype(f32)
        conv[half:, tile_at(i)] = high + skip * second.astype(f32)
        logs = decay_ref[pl.ds(pl.multiple_of(i * per, per), per), :]
        row = jnp.dot(logs, spread, preferred_element_type=f32, precision=lax.Precision.HIGHEST)
        row = jnp.sum(jnp.where(sub == sub_lane, row, 0.0), axis=0, keepdims=True)
        entering[:, tile_at(i)] = jnp.exp(after * row).astype(bf16)
        q_ref[:, tile_at(i)] = short(q_ref, 0, i).astype(bf16)
        return 0

    loads[6].wait()

    carry[...] = jnp.zeros_like(carry)
    half_tiles = tiles // 2
    core = lax.rem(me, 2)
    lead = max(tiles // 8, 1)
    tail = max(tiles // 16, 1)
    bounds = [0] + [lead + (tiles - lead - tail) * r // (rounds - 1) for r in range(rounds)]
    for r in range(rounds):
        bit = 1 << r
        last = r == rounds - 1
        upper = lax.rem(lax.div(me, bit), 2) == 1
        copy = scan_copy(r)
        if last:
            @pl.when(jnp.logical_not(upper))
            def _():
                copy.start()
        else:
            copy.start()
        lax.fori_loop(bounds[r], bounds[r + 1], convolve, 0)
        block_rate = float(tok * bit)
        offset = ((lax.rem(me, bit) - core) * tok).astype(f32) if r else None

        def merge(i, _):
            place = tile_at(core * half_tiles + i)
            theirs = (state_in[r, :, tile_at(i)] if r else first_in[:, place]).astype(f32)
            logs = rate[:, place]
            if r:
                inward = jnp.exp(logs * offset) * theirs
                carry[:, tile_at(i)] += jnp.where(upper, inward, 0.0)
            if not last:
                mine = total[:, place]
                later = jnp.where(upper, mine, theirs)
                before = jnp.where(upper, theirs, mine)
                both = jnp.exp(logs * block_rate) * before + later
                total[:, place] = both
                state_out[r + 1, :, tile_at(i)] = both.astype(bf16)
            return 0

        if last:
            @pl.when(upper)
            def _():
                copy.wait_recv()
                lax.fori_loop(0, half_tiles, merge, 0)
        else:
            copy.wait_recv()
            lax.fori_loop(0, half_tiles, merge, 0)

    share = pltpu.make_async_remote_copy(carry, carry_in, carry_send, carry_recv,
                                         device_id={"seq": partner(1)}, device_id_type=MESH)
    share.start()
    lax.fori_loop(bounds[rounds], tiles, convolve, 0)
    share.wait()

    def assemble(i, _):
        for part, side in ((carry, core), (carry_in, 1 - core)):
            place = tile_at(side * half_tiles + i)
            entry = part[:, tile_at(i)]
            moved = jnp.exp(rate[:, place] * float(tok)) * entry + first_in[:, place].astype(f32)
            total[:, place] = jnp.where(core == 1, moved, entry)
        return 0

    lax.fori_loop(0, half_tiles, assemble, 0)

    square[...] = jnp.zeros_like(square)
    loads[7].wait()

    def gated_tile(i):
        state = total[:, tile_at(i)] * wide_weight[:, tile_at(i)]
        diagonal = jnp.concatenate([jnp.where(lane_group == j, state, 0.0) for j in range(per)], axis=0)
        fine = diagonal.astype(bf16)
        rest = (diagonal - fine.astype(f32)).astype(bf16)
        ent = entering[:, tile_at(i)]
        carried = jnp.dot(jnp.concatenate([ent, ent], axis=1), jnp.concatenate([fine, rest], axis=0),
                          preferred_element_type=f32)
        return q_ref[:, tile_at(i)].astype(f32) * (conv[:, tile_at(i)] + carried)

    def gate(i, _):
        one, two = gated_tile(2 * i), gated_tile(2 * i + 1)
        conv[:, tile_at(2 * i)] = one
        conv[:, tile_at(2 * i + 1)] = two
        square[...] += one * one + two * two
        return 0

    lax.fori_loop(0, tiles // 2, gate, 0)

    sums = jnp.sum(square[...].T, axis=0, keepdims=True)
    square_out[...] = jnp.broadcast_to(sums, square_out.shape)
    copies = []
    for d in range(1, nch):
        c = pltpu.make_async_remote_copy(square_out, square_in.at[d - 1], square_send.at[d - 1], square_recv.at[d - 1],
                                         device_id={"ch": lax.rem(mych + d, nch)}, device_id_type=MESH)
        c.start()
        copies.append(c)
    for d, c in enumerate(copies):
        c.wait()
        sums = sums + square_in[d, 0:1, :]
    scale = lax.rsqrt(sums / (channels * nch) + 1e-5)
    square[...] = jnp.broadcast_to(scale, (LANES, tok)).T

    def finish(i, _):
        out_ref[:, tile_at(i)] = (conv[:, tile_at(i)] * square[...] * gain_ref[:, tile_at(i)]).astype(bf16)
        return 0

    lax.fori_loop(0, tiles, finish, 0)

    @pl.when(me < n - 1)
    def _():
        halo.wait_send()

    for r in range(rounds):
        bit = 1 << r
        copy = scan_copy(r)
        if r == rounds - 1:
            @pl.when(lax.rem(lax.div(me, bit), 2) == 0)
            def _():
                copy.wait_send()
        else:
            copy.wait_send()


def on_device(n, nch, q_proj, k_proj, v_proj, short_filter, log_decay, residue, skip_bias, norm_gain):
    tok, channels = q_proj.shape
    groups, modes = log_decay.shape
    rounds = n.bit_length() - 1
    assert channels % (2 * LANES) == 0 and n == 1 << rounds and rounds > 1 and channels == groups * modes
    vmem = pl.BlockSpec(memory_space=pltpu.VMEM)
    dma = pltpu.SemaphoreType.DMA
    return pl.pallas_call(
        functools.partial(kernel, n, nch, rounds, modes),
        out_shape=jax.ShapeDtypeStruct((tok, channels), bf16),
        in_specs=[pl.BlockSpec(memory_space=pltpu.HBM)] * 8,
        out_specs=vmem,
        scratch_shapes=[
            pltpu.VMEM((tok, channels), bf16),
            pltpu.VMEM((tok, channels), bf16),
            pltpu.VMEM((tok, channels), bf16),
            pltpu.VMEM((9, channels), f32),
            pltpu.VMEM((modes, groups), f32),
            pltpu.VMEM((modes, groups), f32),
            pltpu.VMEM((1, channels), f32),
            pltpu.VMEM((1, channels), f32),
            pltpu.VMEM((3, 16, channels), bf16),
            pltpu.VMEM((groups, modes), f32),
            pltpu.VMEM((groups, modes), f32),
            pltpu.VMEM((8, channels), f32),
            pltpu.VMEM((8, channels), f32),
            pltpu.VMEM((6, tok + 8, LANES), f32),
            pltpu.VMEM((channels, tok), bf16),
            pltpu.VMEM((groups, tok), f32),
            pltpu.VMEM((tok, channels), bf16),
            pltpu.VMEM((tok, channels), bf16),
            pltpu.VMEM((tok, channels), f32),
            pltpu.VMEM((modes, channels), f32),
            pltpu.VMEM((modes, channels), f32),
            pltpu.VMEM((modes, channels), f32),
            pltpu.VMEM((modes, channels // 2), f32),
            pltpu.VMEM((modes, channels // 2), f32),
            pltpu.VMEM((modes, channels), bf16),
            pltpu.VMEM((modes, channels), bf16),
            pltpu.VMEM((rounds, modes, channels // 2), bf16),
            pltpu.VMEM((rounds, modes, channels // 2), bf16),
            pltpu.VMEM((tok, LANES), f32),
            pltpu.VMEM((8, tok), f32),
            pltpu.VMEM((max(nch - 1, 1), 8, tok), f32),
            dma, dma, dma((rounds,)), dma((rounds,)), dma((max(nch - 1, 1),)), dma((max(nch - 1, 1),)),
            dma((8,)), dma((3,)), dma, dma,
        ],
        compiler_params=pltpu.CompilerParams(collective_id=0, has_side_effects=True,
                                             vmem_limit_bytes=56 * 1024 * 1024),
    )(q_proj, k_proj, v_proj, short_filter, log_decay.T, residue.T,
      skip_bias.reshape(1, channels), norm_gain.reshape(1, channels))


def solution(mesh):
    return jax.shard_map(
        functools.partial(on_device, mesh.shape["seq"], mesh.shape["ch"]),
        mesh=mesh,
        in_specs=(P("seq", "ch"), P("seq", "ch"), P("seq", "ch"), P(None, "ch"),
                  P("ch", None), P("ch", None), P("ch"), P("ch")),
        out_specs=P("seq", "ch"),
        check_vma=False,
    )
```

```python
import functools
import jax
import jax.numpy as jnp
from jax import lax
from jax.experimental import pallas as pl
from jax.experimental.pallas import tpu as pltpu
from jax.sharding import PartitionSpec as P

LANES = 128
PARTS = 2
MESH = pl.DeviceIdType.MESH
f32 = jnp.float32
bf16 = jnp.bfloat16


def tile_at(i):
    return pl.ds(pl.multiple_of(i * LANES, LANES), LANES)


def kernel(n, nch, rounds, modes, q_hbm, k_hbm, v_hbm, taps_hbm, decay_hbm, residue_hbm, skip_hbm,
           conv, square, q_ref, k_ref, v_ref, taps_ref, decay_flat, residue_flat, skip_ref,
           tails, decay_ref, residue_ref, halo_out, halo_in, pad, leaving, hrev, entering, mixed, rate, wide_weight,
           total, first_half, carry, carry_in, first_out, first_in, state_out, state_in, square_out, square_in,
           halo_send, halo_recv, state_send, state_recv, square_send, square_recv, load_sem, tail_sem, carry_send, carry_recv):
    tok, channels = q_ref.shape
    half = tok // 2
    tiles = channels // LANES
    part_tiles = tiles // PARTS
    half_tiles = part_tiles // 2
    per = LANES // modes
    me = lax.axis_index("seq")
    mych = lax.axis_index("ch")
    right, left = lax.rem(me + 1, n), lax.rem(me + n - 1, n)

    def partner(bit):
        return me + bit * (1 - 2 * lax.rem(lax.div(me, bit), 2))

    def scan_copy(p, r):
        return pltpu.make_async_remote_copy(
            state_out.at[p, r] if r else first_out.at[p], state_in.at[p, r] if r else first_in.at[p],
            state_send.at[p, r], state_recv.at[p, r], device_id={"seq": partner(1 << r)}, device_id_type=MESH)

    def share_copy(p):
        return pltpu.make_async_remote_copy(carry.at[p], carry_in.at[p], carry_send.at[p], carry_recv.at[p],
                                            device_id={"seq": partner(1)}, device_id_type=MESH)

    order = ((decay_hbm, decay_flat), (residue_hbm, residue_flat), (k_hbm, k_ref), (v_hbm, v_ref), (taps_hbm, taps_ref),
             (skip_hbm, skip_ref), (q_hbm, q_ref))
    tail_loads = [pltpu.make_async_copy(ref.at[tok - 16:tok, :], tails.at[j], tail_sem.at[j])
                  for j, ref in enumerate((q_hbm, k_hbm, v_hbm))]
    loads = [pltpu.make_async_copy(src, dst, load_sem.at[j]) for j, (src, dst) in enumerate(order)]
    for load in tail_loads + loads:
        load.start()
    barrier = pltpu.get_barrier_semaphore()
    for other in [right, left] + [partner(1 << r) for r in range(rounds)]:
        pl.semaphore_signal(barrier, inc=1, device_id={"seq": other}, device_id_type=MESH)
    for d in range(1, nch):
        pl.semaphore_signal(barrier, inc=1, device_id={"ch": lax.rem(mych + d, nch)}, device_id_type=MESH)

    for load in tail_loads:
        load.wait()

    def make_halo(i, _):
        last = [tails[j, :, tile_at(i)].astype(f32)[14:16] for j in range(3)]
        halo_out[:, tile_at(i)] = jnp.concatenate(last + [jnp.zeros((2, LANES), f32)], axis=0).astype(bf16)
        return 0

    lax.fori_loop(0, tiles, make_halo, 0, unroll=4)
    pl.semaphore_wait(barrier, 2 + rounds + nch - 1)

    halo = pltpu.make_async_remote_copy(halo_out, halo_in, halo_send, halo_recv,
                                        device_id={"seq": right}, device_id_type=MESH)

    @pl.when(me < n - 1)
    def _():
        halo.start()

    lane = lax.broadcasted_iota(jnp.int32, (1, LANES), 1)
    lane_group = lane // modes
    lags_rev = (half - 1 - lax.broadcasted_iota(jnp.int32, (1, half), 1)).astype(f32)
    after = (lax.broadcasted_iota(jnp.int32, (half, 1), 0) + 1).astype(f32)
    own_mode = (lax.broadcasted_iota(jnp.int32, (modes, LANES), 1) % modes
                == lax.broadcasted_iota(jnp.int32, (modes, LANES), 0))

    def prepare(i, _):
        logs = decay_ref[pl.ds(pl.multiple_of(i * per, per), per), :]
        res = residue_ref[pl.ds(pl.multiple_of(i * per, per), per), :]
        pole = jnp.exp(logs)
        weight = res * jnp.sqrt(1.0 - pole * pole)
        cols, wcols = logs.T, weight.T
        rows = []
        wide_rate = jnp.zeros((modes, LANES), f32)
        wide_w = jnp.zeros((modes, LANES), f32)
        for j in range(per):
            col = jnp.broadcast_to(cols[:, j:j + 1], (modes, LANES))
            wcol = jnp.broadcast_to(wcols[:, j:j + 1], (modes, LANES))
            power = jnp.exp(col * lags_rev)
            leaving[pl.ds(pl.multiple_of(i * LANES, LANES) + j * modes, modes), :] = power.astype(bf16)
            rows.append(jnp.sum(power * wcol, axis=0, keepdims=True))
            wide_rate = jnp.where(lane_group == j, col, wide_rate)
            wide_w = jnp.where(lane_group == j, wcol, wide_w)
        hrev[pl.ds(pl.multiple_of(i * per, per), per), :] = jnp.concatenate(rows, axis=0)
        rate[:, tile_at(i)] = wide_rate
        wide_weight[:, tile_at(i)] = wide_w
        return 0

    loads[0].wait()
    loads[1].wait()
    decay_ref[...] = decay_flat[...].T
    residue_ref[...] = residue_flat[...].T
    lax.fori_loop(0, tiles, prepare, 0)
    for load in loads[2:6]:
        load.wait()

    @pl.when(me > 0)
    def _():
        halo.wait_recv()

    @pl.when(me == 0)
    def _():
        halo_in[...] = jnp.zeros_like(halo_in)

    def short(ref, which, i, slot=0):
        place = 3 * slot + which
        x = ref[:, tile_at(i)].astype(f32)
        pad[place, 8:8 + tok, :] = x
        before = halo_in[:, tile_at(i)].astype(f32)
        pad[place, 0:8, :] = pltpu.roll(before, 6 - 2 * which, 0) if which < 3 else before
        a = [taps_ref[3 * which + t:3 * which + t + 1, tile_at(i)] for t in range(3)]
        return a[0] * x + a[1] * pad[place, 7:7 + tok, :] + a[2] * pad[place, 6:6 + tok, :]

    def pick(stacked):
        out = stacked[0:modes]
        for j in range(1, per):
            out = jnp.where(lane_group == j, stacked[j * modes:(j + 1) * modes], out)
        return out

    def summarize(p):
        def body(i, _):
            pair = [2 * i, 2 * i + 1]
            values = [(short(k_ref, 1, t, u) * short(v_ref, 2, t, u)).astype(bf16) for u, t in enumerate(pair)]
            for u, t in enumerate(pair):
                mixed[:, tile_at(t)] = values[u]
                sides = jnp.concatenate([values[u][:half], values[u][half:]], axis=1)
                spread = jnp.dot(leaving[tile_at(t), :], sides, preferred_element_type=f32)
                one, two = pick(spread[:, :LANES]), pick(spread[:, LANES:])
                state = jnp.exp(rate[:, tile_at(t)] * float(half)) * one + two
                first_half[:, tile_at(t)] = one
                total[:, tile_at(t)] = state
                first_out[p, :, tile_at(t - p * part_tiles)] = state.astype(bf16)
            return 0

        lax.fori_loop(p * part_tiles // 2, (p + 1) * part_tiles // 2, body, 0)

    for p in range(PARTS):
        summarize(p)
        scan_copy(p, 0).start()

    causal = (lax.broadcasted_iota(jnp.int32, (half, LANES), 1)
              <= lax.broadcasted_iota(jnp.int32, (half, LANES), 0))

    def diagonal(state):
        fine = state.astype(bf16).astype(f32)
        return jnp.concatenate([jnp.where(lane_group == j, fine, 0.0) for j in range(per)], axis=0).astype(bf16)

    def convolve(i, _):
        values = mixed[:, tile_at(i)]
        first, second = values[:half], values[half:]
        sides = jnp.concatenate([first, second], axis=1)
        row = jnp.sum(jnp.where(own_mode, rate[:, tile_at(i)], 0.0), axis=0, keepdims=True)
        ent = jnp.exp(after * row).astype(bf16)
        entering[:, tile_at(i)] = ent
        lines = hrev[pl.ds(pl.multiple_of(i * per, per), per), :]
        left_side, right_side = [], []
        both_groups = jnp.concatenate([lane_group, lane_group], axis=1)
        for j in range(per):
            line = jnp.broadcast_to(lines[j:j + 1], (half, LANES))
            block = pltpu.roll(line, 1, 1, stride=1, stride_axis=0)
            left_side.append(jnp.where(causal, block, 0.0).astype(bf16))
            right_side.append(jnp.where(both_groups == j, sides, jnp.zeros_like(sides)))
        state = diagonal(first_half[:, tile_at(i)] * wide_weight[:, tile_at(i)])
        left_side.append(ent)
        right_side.append(jnp.concatenate([jnp.zeros_like(state), state], axis=1))
        product = jnp.dot(jnp.concatenate(left_side, axis=1), jnp.concatenate(right_side, axis=0),
                          preferred_element_type=f32)
        skip = skip_ref[:, tile_at(i)]
        conv[:half, tile_at(i)] = product[:, :LANES] + skip * first.astype(f32)
        conv[half:, tile_at(i)] = product[:, LANES:] + skip * second.astype(f32)
        q_ref[:, tile_at(i)] = short(q_ref, 0, i).astype(bf16)
        return 0

    loads[6].wait()

    carry[...] = jnp.zeros_like(carry)
    core = lax.rem(me, 2)
    weights = [max(tiles // 16, 1)] + [tiles] * (rounds - 1)
    lead = weights[0]
    bounds = [0] + [lead + (tiles - lead) * r // (rounds - 1) for r in range(rounds)]
    for r in range(rounds):
        bit = 1 << r
        last = r == rounds - 1
        upper = lax.rem(lax.div(me, bit), 2) == 1
        lax.fori_loop(bounds[r], bounds[r + 1], convolve, 0)
        block_rate = float(tok * bit)
        offset = ((lax.rem(me, bit) - core) * tok).astype(f32) if r else None

        def merge(p, i):
            local = core * half_tiles + i
            place = tile_at(p * part_tiles + local)
            theirs = (state_in[p, r, :, tile_at(i)] if r else first_in[p, :, tile_at(local)]).astype(f32)
            logs = rate[:, place]
            if r:
                inward = jnp.exp(logs * offset) * theirs
                carry[p, :, tile_at(i)] += jnp.where(upper, inward, 0.0)
            if not last:
                mine = total[:, place]
                later = jnp.where(upper, mine, theirs)
                before = jnp.where(upper, theirs, mine)
                both = jnp.exp(logs * block_rate) * before + later
                total[:, place] = both
                state_out[p, r + 1, :, tile_at(i)] = both.astype(bf16)

        def arrive(p):
            scan_copy(p, r).wait_recv()

            def body(i, _):
                merge(p, i)
                return 0

            lax.fori_loop(0, half_tiles, body, 0, unroll=4)

        for p in range(PARTS):
            if last:
                @pl.when(upper)
                def _():
                    arrive(p)

                share_copy(p).start()
            else:
                arrive(p)
                following = scan_copy(p, r + 1)
                if r + 1 == rounds - 1:
                    @pl.when(lax.rem(lax.div(me, 2 * bit), 2) == 0)
                    def _():
                        following.start()
                else:
                    following.start()

    def assemble(p):
        def body(i, _):
            for part, side in ((carry, core), (carry_in, 1 - core)):
                local = side * half_tiles + i
                place = tile_at(p * part_tiles + local)
                entry = part[p, :, tile_at(i)]
                moved = jnp.exp(rate[:, place] * float(tok)) * entry + first_in[p, :, tile_at(local)].astype(f32)
                total[:, place] = jnp.where(core == 1, moved, entry)
            return 0

        lax.fori_loop(0, half_tiles, body, 0, unroll=2)

    square[...] = jnp.zeros_like(square)

    def gated_tile(i):
        state = total[:, tile_at(i)] * wide_weight[:, tile_at(i)]
        later = state * jnp.exp(rate[:, tile_at(i)] * float(half))
        columns = []
        for s in (state, later):
            fine = s.astype(bf16).astype(f32)
            columns.append(jnp.concatenate([diagonal(fine), diagonal(s - fine)], axis=0))
        ent = entering[:, tile_at(i)]
        carried = jnp.dot(jnp.concatenate([ent, ent], axis=1), jnp.concatenate(columns, axis=1),
                          preferred_element_type=f32)
        gated = []
        for side in range(2):
            rows = slice(side * half, (side + 1) * half)
            g = q_ref[rows, tile_at(i)].astype(f32) * (conv[rows, tile_at(i)] + carried[:, side * LANES:(side + 1) * LANES])
            conv[rows, tile_at(i)] = g
            gated.append(g)
        return gated

    def gate(i, _):
        one, two = gated_tile(2 * i), gated_tile(2 * i + 1)
        for side in range(2):
            rows = slice(side * half, (side + 1) * half)
            square[rows, :] += one[side] * one[side] + two[side] * two[side]
        return 0

    for p in range(PARTS):
        share_copy(p).wait()
        assemble(p)
        lax.fori_loop(p * part_tiles // 2, (p + 1) * part_tiles // 2, gate, 0)

    sums = jnp.sum(square[...].T, axis=0, keepdims=True)
    square_out[...] = jnp.broadcast_to(sums, square_out.shape)
    copies = []
    for d in range(1, nch):
        c = pltpu.make_async_remote_copy(square_out, square_in.at[d - 1], square_send.at[d - 1], square_recv.at[d - 1],
                                         device_id={"ch": lax.rem(mych + d, nch)}, device_id_type=MESH)
        c.start()
        copies.append(c)
    for d, c in enumerate(copies):
        c.wait()
        sums = sums + square_in[d, 0:1, :]
    scale = lax.rsqrt(sums / (channels * nch) + 1e-5)
    square[...] = jnp.broadcast_to(scale, (LANES, tok)).T

    @pl.when(me < n - 1)
    def _():
        halo.wait_send()

    for p in range(PARTS):
        for r in range(rounds):
            bit = 1 << r
            copy = scan_copy(p, r)
            if r == rounds - 1:
                @pl.when(lax.rem(lax.div(me, bit), 2) == 0)
                def _():
                    copy.wait_send()
            else:
                copy.wait_send()


def normalize(gated_ref, scale_ref, gain_ref, out_hbm, out_ref, sem):
    pieces = out_ref.shape[0]
    width = out_ref.shape[2]

    def copy(j):
        return pltpu.make_async_copy(out_ref.at[j], out_hbm.at[:, j * width:(j + 1) * width], sem.at[j])

    for j in range(pieces):
        for i in range(width // LANES):
            place = slice(j * width + i * LANES, j * width + (i + 1) * LANES)
            out_ref[j, :, i * LANES:(i + 1) * LANES] = (gated_ref[:, place] * scale_ref[...] * gain_ref[:, place]).astype(bf16)
        copy(j).start()
    for j in range(pieces):
        copy(j).wait()


def on_device(n, nch, q_proj, k_proj, v_proj, short_filter, log_decay, residue, skip_bias, norm_gain):
    tok, channels = q_proj.shape
    groups, modes = log_decay.shape
    rounds = n.bit_length() - 1
    assert channels % (4 * PARTS * LANES) == 0 and n == 1 << rounds and rounds > 1 and channels == groups * modes
    vmem = pl.BlockSpec(memory_space=pltpu.VMEM)
    dma = pltpu.SemaphoreType.DMA
    part = channels // PARTS
    gated, scale = pl.pallas_call(
        functools.partial(kernel, n, nch, rounds, modes),
        out_shape=(jax.ShapeDtypeStruct((tok, channels), f32), jax.ShapeDtypeStruct((tok, LANES), f32)),
        in_specs=[pl.BlockSpec(memory_space=pltpu.HBM)] * 7,
        out_specs=(vmem, vmem),
        scratch_shapes=[
            pltpu.VMEM((tok, channels), bf16),
            pltpu.VMEM((tok, channels), bf16),
            pltpu.VMEM((tok, channels), bf16),
            pltpu.VMEM((9, channels), f32),
            pltpu.VMEM((modes, groups), f32),
            pltpu.VMEM((modes, groups), f32),
            pltpu.VMEM((1, channels), f32),
            pltpu.VMEM((3, 16, channels), bf16),
            pltpu.VMEM((groups, modes), f32),
            pltpu.VMEM((groups, modes), f32),
            pltpu.VMEM((8, channels), bf16),
            pltpu.VMEM((8, channels), bf16),
            pltpu.VMEM((6, tok + 8, LANES), f32),
            pltpu.VMEM((channels, tok // 2), bf16),
            pltpu.VMEM((groups, tok // 2), f32),
            pltpu.VMEM((tok // 2, channels), bf16),
            pltpu.VMEM((tok, channels), bf16),
            pltpu.VMEM((modes, channels), f32),
            pltpu.VMEM((modes, channels), f32),
            pltpu.VMEM((modes, channels), f32),
            pltpu.VMEM((modes, channels), f32),
            pltpu.VMEM((PARTS, modes, part // 2), f32),
            pltpu.VMEM((PARTS, modes, part // 2), f32),
            pltpu.VMEM((PARTS, modes, part), bf16),
            pltpu.VMEM((PARTS, modes, part), bf16),
            pltpu.VMEM((PARTS, rounds, modes, part // 2), bf16),
            pltpu.VMEM((PARTS, rounds, modes, part // 2), bf16),
            pltpu.VMEM((8, tok), f32),
            pltpu.VMEM((max(nch - 1, 1), 8, tok), f32),
            dma, dma, dma((PARTS, rounds)), dma((PARTS, rounds)), dma((max(nch - 1, 1),)), dma((max(nch - 1, 1),)),
            dma((7,)), dma((3,)), dma((PARTS,)), dma((PARTS,)),
        ],
        compiler_params=pltpu.CompilerParams(collective_id=0, has_side_effects=True,
                                             vmem_limit_bytes=LIMIT_A),
    )(*[pltpu.with_memory_space_constraint(x, pltpu.HBM) for x in (q_proj, k_proj, v_proj, short_filter, log_decay.T, residue.T, skip_bias.reshape(1, channels))])
    pieces = 8
    return pl.pallas_call(
        normalize,
        out_shape=jax.ShapeDtypeStruct((tok, channels), bf16),
        in_specs=[vmem, vmem, vmem],
        out_specs=pl.BlockSpec(memory_space=pltpu.HBM),
        scratch_shapes=[pltpu.VMEM((pieces, tok, channels // pieces), bf16), dma((pieces,))],
        compiler_params=pltpu.CompilerParams(vmem_limit_bytes=LIMIT_B),
    )(gated, scale, norm_gain.reshape(1, channels))


LIMIT_A = 28 * 1024 * 1024
LIMIT_B = 16 * 1024 * 1024


def solution(mesh):
    return jax.shard_map(
        functools.partial(on_device, mesh.shape["seq"], mesh.shape["ch"]),
        mesh=mesh,
        in_specs=(P("seq", "ch"), P("seq", "ch"), P("seq", "ch"), P(None, "ch"),
                  P("ch", None), P("ch", None), P("ch"), P("ch")),
        out_specs=P("seq", "ch"),
        check_vma=False,
    )
```

```python
import functools
import jax
import jax.numpy as jnp
from jax import lax
from jax.experimental import pallas as pl
from jax.experimental.pallas import tpu as pltpu
from jax.sharding import PartitionSpec as P

LANES = 128
PARTS = 2
MESH = pl.DeviceIdType.MESH
f32 = jnp.float32
LOG2E = 1.4426950408889634
bf16 = jnp.bfloat16


def tile_at(i):
    return pl.ds(pl.multiple_of(i * LANES, LANES), LANES)


def kernel(n, nch, rounds, modes, q_hbm, k_hbm, v_hbm, taps_hbm, decay_hbm, residue_hbm, skip_hbm,
           conv, square, q_ref, k_ref, v_ref, taps_ref, decay_flat, residue_flat, skip_ref,
           tails, halo_out, halo_in, pad, leaving, hrev, entering, mixed, rate, wide_weight,
           total, first_half, carry, carry_in, first_out, first_in, state_out, state_in, square_out, square_in,
           halo_send, halo_recv, state_send, state_recv, square_send, square_recv, load_sem, tail_sem, carry_send, carry_recv):
    tok, channels = q_ref.shape
    half = tok // 2
    tiles = channels // LANES
    part_tiles = tiles // PARTS
    half_tiles = part_tiles // 2
    per = LANES // modes
    me = lax.axis_index("seq")
    mych = lax.axis_index("ch")
    right, left = lax.rem(me + 1, n), lax.rem(me + n - 1, n)

    def partner(bit):
        return me + bit * (1 - 2 * lax.rem(lax.div(me, bit), 2))

    def scan_copy(p, r):
        return pltpu.make_async_remote_copy(
            state_out.at[p, r] if r else first_out.at[p], state_in.at[p, r] if r else first_in.at[p],
            state_send.at[p, r], state_recv.at[p, r], device_id={"seq": partner(1 << r)}, device_id_type=MESH)

    def share_copy(p):
        return pltpu.make_async_remote_copy(carry.at[p], carry_in.at[p], carry_send.at[p], carry_recv.at[p],
                                            device_id={"seq": partner(1)}, device_id_type=MESH)

    order = ((decay_hbm, decay_flat), (residue_hbm, residue_flat), (k_hbm, k_ref), (v_hbm, v_ref), (taps_hbm, taps_ref),
             (skip_hbm, skip_ref), (q_hbm, q_ref))
    tail_loads = [pltpu.make_async_copy(ref.at[tok - 16:tok, :], tails.at[j], tail_sem.at[j])
                  for j, ref in enumerate((q_hbm, k_hbm, v_hbm))]
    loads = [pltpu.make_async_copy(src, dst, load_sem.at[j]) for j, (src, dst) in enumerate(order)]
    for load in tail_loads + loads:
        load.start()
    barrier = pltpu.get_barrier_semaphore()
    for other in [right, left] + [partner(1 << r) for r in range(rounds)]:
        pl.semaphore_signal(barrier, inc=1, device_id={"seq": other}, device_id_type=MESH)
    for d in range(1, nch):
        pl.semaphore_signal(barrier, inc=1, device_id={"ch": lax.rem(mych + d, nch)}, device_id_type=MESH)

    for load in tail_loads:
        load.wait()

    def make_halo(i, _):
        last = [tails[j, :, tile_at(i)].astype(f32)[14:16] for j in range(3)]
        halo_out[:, tile_at(i)] = jnp.concatenate(last + [jnp.zeros((2, LANES), f32)], axis=0).astype(bf16)
        return 0

    lax.fori_loop(0, tiles, make_halo, 0, unroll=4)
    pl.semaphore_wait(barrier, 2 + rounds + nch - 1)

    halo = pltpu.make_async_remote_copy(halo_out, halo_in, halo_send, halo_recv,
                                        device_id={"seq": right}, device_id_type=MESH)

    @pl.when(me < n - 1)
    def _():
        halo.start()

    lane = lax.broadcasted_iota(jnp.int32, (1, LANES), 1)
    lane_group = lane // modes
    lags_rev = (half - 1 - lax.broadcasted_iota(jnp.int32, (1, half), 1)).astype(f32)
    after = (lax.broadcasted_iota(jnp.int32, (half, 1), 0) + 1).astype(f32)
    own_mode = (lax.broadcasted_iota(jnp.int32, (modes, LANES), 1) % modes
                == lax.broadcasted_iota(jnp.int32, (modes, LANES), 0))

    group_row = lax.broadcasted_iota(jnp.int32, (per, LANES), 0)
    blocks = LANES // per

    def prepare(i, _):
        block = tile_at(lax.div(i, blocks))
        index = jnp.broadcast_to(per * lax.rem(i, blocks) + lane_group, (modes, LANES))
        wide_rate = jnp.take_along_axis(decay_flat[:, block], index, axis=1)
        wide_w = jnp.take_along_axis(residue_flat[:, block], index, axis=1)
        rate[:, tile_at(i)] = wide_rate
        wide_weight[:, tile_at(i)] = wide_w
        powers = []
        for j in range(per):
            col = wide_rate[:, j * modes:j * modes + 1]
            powers.append(jnp.exp2(col * lags_rev).astype(bf16))
        powers = jnp.concatenate(powers, axis=0)
        leaving[tile_at(i), :] = powers
        row = jnp.sum(jnp.where(own_mode, wide_rate, 0.0), axis=0, keepdims=True)
        wrow = jnp.sum(jnp.where(own_mode, wide_w, 0.0), axis=0, keepdims=True)
        spread_w = jnp.where(group_row == lane_group, wrow, 0.0)
        coarse = spread_w.astype(bf16).astype(f32)
        both = jnp.dot(jnp.concatenate([coarse, spread_w - coarse], axis=0).astype(bf16), powers, preferred_element_type=f32)
        hrev[pl.ds(pl.multiple_of(i * per, per), per), :] = both[:per] + both[per:]
        entering[:, tile_at(i)] = jnp.exp2(after * row).astype(bf16)
        return 0

    loads[0].wait()
    loads[1].wait()
    pole = jnp.exp(decay_flat[...])
    residue_flat[...] = residue_flat[...] * jnp.sqrt(1.0 - pole * pole)
    decay_flat[...] = decay_flat[...] * LOG2E
    lax.fori_loop(0, tiles, prepare, 0, unroll=UP)
    for load in loads[2:6]:
        load.wait()

    @pl.when(me > 0)
    def _():
        halo.wait_recv()

    @pl.when(me == 0)
    def _():
        halo_in[...] = jnp.zeros_like(halo_in)

    def short(ref, which, i, slot=0):
        place = 3 * slot + which
        x = ref[:, tile_at(i)].astype(f32)
        pad[place, 8:8 + tok, :] = x
        before = halo_in[:, tile_at(i)].astype(f32)
        pad[place, 0:8, :] = pltpu.roll(before, 6 - 2 * which, 0) if which < 3 else before
        a = [taps_ref[3 * which + t:3 * which + t + 1, tile_at(i)] for t in range(3)]
        return a[0] * x + a[1] * pad[place, 7:7 + tok, :] + a[2] * pad[place, 6:6 + tok, :]

    def pick(stacked):
        out = stacked[0:modes]
        for j in range(1, per):
            out = jnp.where(lane_group == j, stacked[j * modes:(j + 1) * modes], out)
        return out

    def summarize(p):
        def body(i, _):
            pair = [2 * i, 2 * i + 1]
            values = [(short(k_ref, 1, t, u) * short(v_ref, 2, t, u)).astype(bf16) for u, t in enumerate(pair)]
            for u, t in enumerate(pair):
                mixed[:, tile_at(t)] = values[u]
                sides = jnp.concatenate([values[u][:half], values[u][half:]], axis=1)
                spread = jnp.dot(leaving[tile_at(t), :], sides, preferred_element_type=f32)
                one, two = pick(spread[:, :LANES]), pick(spread[:, LANES:])
                state = jnp.exp2(rate[:, tile_at(t)] * float(half)) * one + two
                first_half[:, tile_at(t)] = one
                total[:, tile_at(t)] = state
                first_out[p, :, tile_at(t - p * part_tiles)] = state.astype(bf16)
            return 0

        lax.fori_loop(p * part_tiles // 2, (p + 1) * part_tiles // 2, body, 0)

    for p in range(PARTS):
        summarize(p)
        scan_copy(p, 0).start()

    causal = (lax.broadcasted_iota(jnp.int32, (half, LANES), 1)
              <= lax.broadcasted_iota(jnp.int32, (half, LANES), 0))

    def diagonal(state):
        fine = state.astype(bf16).astype(f32)
        return jnp.concatenate([jnp.where(lane_group == j, fine, 0.0) for j in range(per)], axis=0).astype(bf16)

    def convolve(i, _):
        values = mixed[:, tile_at(i)]
        first, second = values[:half], values[half:]
        sides = jnp.concatenate([first, second], axis=1)
        ent = entering[:, tile_at(i)]
        lines = hrev[pl.ds(pl.multiple_of(i * per, per), per), :]
        left_side, right_side = [], []
        both_groups = jnp.concatenate([lane_group, lane_group], axis=1)
        for j in range(per):
            line = jnp.broadcast_to(lines[j:j + 1], (half, LANES))
            block = pltpu.roll(line, 1, 1, stride=1, stride_axis=0)
            left_side.append(jnp.where(causal, block, 0.0).astype(bf16))
            right_side.append(jnp.where(both_groups == j, sides, jnp.zeros_like(sides)))
        state = diagonal(first_half[:, tile_at(i)] * wide_weight[:, tile_at(i)])
        left_side.append(ent)
        right_side.append(jnp.concatenate([jnp.zeros_like(state), state], axis=1))
        product = jnp.dot(jnp.concatenate(left_side, axis=1), jnp.concatenate(right_side, axis=0),
                          preferred_element_type=f32)
        skip = skip_ref[:, tile_at(i)]
        conv[:half, tile_at(i)] = product[:, :LANES] + skip * first.astype(f32)
        conv[half:, tile_at(i)] = product[:, LANES:] + skip * second.astype(f32)
        q_ref[:, tile_at(i)] = short(q_ref, 0, i).astype(bf16)
        return 0

    loads[6].wait()

    carry[...] = jnp.zeros_like(carry)
    core = lax.rem(me, 2)
    weights = [max(tiles // 16, 1)] + [tiles] * (rounds - 1)
    lead = weights[0]
    bounds = [0] + [lead + (tiles - lead) * r // (rounds - 1) for r in range(rounds)]
    for r in range(rounds):
        bit = 1 << r
        last = r == rounds - 1
        upper = lax.rem(lax.div(me, bit), 2) == 1
        lax.fori_loop(bounds[r], bounds[r + 1], convolve, 0)
        block_rate = float(tok * bit)
        offset = ((lax.rem(me, bit) - core) * tok).astype(f32) if r else None

        def merge(p, i):
            local = core * half_tiles + i
            place = tile_at(p * part_tiles + local)
            theirs = (state_in[p, r, :, tile_at(i)] if r else first_in[p, :, tile_at(local)]).astype(f32)
            logs = rate[:, place]
            if r:
                inward = jnp.exp2(logs * offset) * theirs
                carry[p, :, tile_at(i)] += jnp.where(upper, inward, 0.0)
            if not last:
                mine = total[:, place]
                later = jnp.where(upper, mine, theirs)
                before = jnp.where(upper, theirs, mine)
                both = jnp.exp2(logs * block_rate) * before + later
                total[:, place] = both
                state_out[p, r + 1, :, tile_at(i)] = both.astype(bf16)

        def arrive(p):
            scan_copy(p, r).wait_recv()

            def body(i, _):
                merge(p, i)
                return 0

            lax.fori_loop(0, half_tiles, body, 0, unroll=4)

        for p in range(PARTS):
            if last:
                @pl.when(upper)
                def _():
                    arrive(p)

                share_copy(p).start()
            else:
                arrive(p)
                following = scan_copy(p, r + 1)
                if r + 1 == rounds - 1:
                    @pl.when(lax.rem(lax.div(me, 2 * bit), 2) == 0)
                    def _():
                        following.start()
                else:
                    following.start()

    def assemble(p):
        def body(i, _):
            for part, side in ((carry, core), (carry_in, 1 - core)):
                local = side * half_tiles + i
                place = tile_at(p * part_tiles + local)
                entry = part[p, :, tile_at(i)]
                moved = jnp.exp2(rate[:, place] * float(tok)) * entry + first_in[p, :, tile_at(local)].astype(f32)
                total[:, place] = jnp.where(core == 1, moved, entry)
            return 0

        lax.fori_loop(0, half_tiles, body, 0, unroll=2)

    square[...] = jnp.zeros_like(square)

    def gated_tile(i):
        state = total[:, tile_at(i)] * wide_weight[:, tile_at(i)]
        later = state * jnp.exp2(rate[:, tile_at(i)] * float(half))
        columns = []
        for s in (state, later):
            fine = s.astype(bf16).astype(f32)
            columns.append(jnp.concatenate([diagonal(fine), diagonal(s - fine)], axis=0))
        ent = entering[:, tile_at(i)]
        carried = jnp.dot(jnp.concatenate([ent, ent], axis=1), jnp.concatenate(columns, axis=1),
                          preferred_element_type=f32)
        gated = []
        for side in range(2):
            rows = slice(side * half, (side + 1) * half)
            g = q_ref[rows, tile_at(i)].astype(f32) * (conv[rows, tile_at(i)] + carried[:, side * LANES:(side + 1) * LANES])
            conv[rows, tile_at(i)] = g
            gated.append(g)
        return gated

    def gate(i, _):
        one, two = gated_tile(2 * i), gated_tile(2 * i + 1)
        for side in range(2):
            rows = slice(side * half, (side + 1) * half)
            square[rows, :] += one[side] * one[side] + two[side] * two[side]
        return 0

    for p in range(PARTS):
        share_copy(p).wait()
        assemble(p)
        lax.fori_loop(p * part_tiles // 2, (p + 1) * part_tiles // 2, gate, 0)

    sums = jnp.sum(square[...].T, axis=0, keepdims=True)
    square_out[...] = jnp.broadcast_to(sums, square_out.shape)
    copies = []
    for d in range(1, nch):
        c = pltpu.make_async_remote_copy(square_out, square_in.at[d - 1], square_send.at[d - 1], square_recv.at[d - 1],
                                         device_id={"ch": lax.rem(mych + d, nch)}, device_id_type=MESH)
        c.start()
        copies.append(c)
    for d, c in enumerate(copies):
        c.wait()
        sums = sums + square_in[d, 0:1, :]
    scale = lax.rsqrt(sums / (channels * nch) + 1e-5)
    square[...] = jnp.broadcast_to(scale, (LANES, tok)).T

    @pl.when(me < n - 1)
    def _():
        halo.wait_send()

    for p in range(PARTS):
        for r in range(rounds):
            bit = 1 << r
            copy = scan_copy(p, r)
            if r == rounds - 1:
                @pl.when(lax.rem(lax.div(me, bit), 2) == 0)
                def _():
                    copy.wait_send()
            else:
                copy.wait_send()


def normalize(gated_ref, scale_ref, gain_ref, out_hbm, out_ref, sem):
    pieces = out_ref.shape[0]
    width = out_ref.shape[2]

    def copy(j):
        return pltpu.make_async_copy(out_ref.at[j], out_hbm.at[:, j * width:(j + 1) * width], sem.at[j])

    for j in range(pieces):
        for i in range(width // LANES):
            place = slice(j * width + i * LANES, j * width + (i + 1) * LANES)
            out_ref[j, :, i * LANES:(i + 1) * LANES] = (gated_ref[:, place] * scale_ref[...] * gain_ref[:, place]).astype(bf16)
        copy(j).start()
    for j in range(pieces):
        copy(j).wait()


def on_device(n, nch, q_proj, k_proj, v_proj, short_filter, log_decay, residue, skip_bias, norm_gain):
    tok, channels = q_proj.shape
    groups, modes = log_decay.shape
    rounds = n.bit_length() - 1
    assert channels % (4 * PARTS * LANES) == 0 and n == 1 << rounds and rounds > 1 and channels == groups * modes
    vmem = pl.BlockSpec(memory_space=pltpu.VMEM)
    dma = pltpu.SemaphoreType.DMA
    part = channels // PARTS
    gated, scale = pl.pallas_call(
        functools.partial(kernel, n, nch, rounds, modes),
        out_shape=(jax.ShapeDtypeStruct((tok, channels), f32), jax.ShapeDtypeStruct((tok, LANES), f32)),
        in_specs=[pl.BlockSpec(memory_space=pltpu.HBM)] * 7,
        out_specs=(vmem, vmem),
        scratch_shapes=[
            pltpu.VMEM((tok, channels), bf16),
            pltpu.VMEM((tok, channels), bf16),
            pltpu.VMEM((tok, channels), bf16),
            pltpu.VMEM((9, channels), f32),
            pltpu.VMEM((modes, groups), f32),
            pltpu.VMEM((modes, groups), f32),
            pltpu.VMEM((1, channels), f32),
            pltpu.VMEM((3, 16, channels), bf16),
            pltpu.VMEM((8, channels), bf16),
            pltpu.VMEM((8, channels), bf16),
            pltpu.VMEM((6, tok + 8, LANES), f32),
            pltpu.VMEM((channels, tok // 2), bf16),
            pltpu.VMEM((groups, tok // 2), f32),
            pltpu.VMEM((tok // 2, channels), bf16),
            pltpu.VMEM((tok, channels), bf16),
            pltpu.VMEM((modes, channels), f32),
            pltpu.VMEM((modes, channels), f32),
            pltpu.VMEM((modes, channels), f32),
            pltpu.VMEM((modes, channels), f32),
            pltpu.VMEM((PARTS, modes, part // 2), f32),
            pltpu.VMEM((PARTS, modes, part // 2), f32),
            pltpu.VMEM((PARTS, modes, part), bf16),
            pltpu.VMEM((PARTS, modes, part), bf16),
            pltpu.VMEM((PARTS, rounds, modes, part // 2), bf16),
            pltpu.VMEM((PARTS, rounds, modes, part // 2), bf16),
            pltpu.VMEM((8, tok), f32),
            pltpu.VMEM((max(nch - 1, 1), 8, tok), f32),
            dma, dma, dma((PARTS, rounds)), dma((PARTS, rounds)), dma((max(nch - 1, 1),)), dma((max(nch - 1, 1),)),
            dma((7,)), dma((3,)), dma((PARTS,)), dma((PARTS,)),
        ],
        compiler_params=pltpu.CompilerParams(collective_id=0, has_side_effects=True,
                                             vmem_limit_bytes=LIMIT_A),
    )(*[pltpu.with_memory_space_constraint(x, pltpu.HBM) for x in (q_proj, k_proj, v_proj, short_filter, log_decay.T, residue.T, skip_bias.reshape(1, channels))])
    pieces = 8
    return pl.pallas_call(
        normalize,
        out_shape=jax.ShapeDtypeStruct((tok, channels), bf16),
        in_specs=[vmem, vmem, vmem],
        out_specs=pl.BlockSpec(memory_space=pltpu.HBM),
        scratch_shapes=[pltpu.VMEM((pieces, tok, channels // pieces), bf16), dma((pieces,))],
        compiler_params=pltpu.CompilerParams(vmem_limit_bytes=LIMIT_B),
    )(gated, scale, norm_gain.reshape(1, channels))


UP = 8
LIMIT_A = 28 * 1024 * 1024
LIMIT_B = 16 * 1024 * 1024


def solution(mesh):
    return jax.shard_map(
        functools.partial(on_device, mesh.shape["seq"], mesh.shape["ch"]),
        mesh=mesh,
        in_specs=(P("seq", "ch"), P("seq", "ch"), P("seq", "ch"), P(None, "ch"),
                  P("ch", None), P("ch", None), P("ch"), P("ch")),
        out_specs=P("seq", "ch"),
        check_vma=False,
    )
```

```python
import functools
import jax
import jax.numpy as jnp
from jax import lax
from jax.experimental import pallas as pl
from jax.experimental.pallas import tpu as pltpu
from jax.sharding import PartitionSpec as P

LANES = 128
MOST_PARTS = 4
MESH = pl.DeviceIdType.MESH
f32 = jnp.float32
LOG2E = 1.4426950408889634
bf16 = jnp.bfloat16


def tile_at(i):
    return pl.ds(pl.multiple_of(i * LANES, LANES), LANES)


def kernel(n, nch, rounds, modes, q_hbm, k_hbm, v_hbm, taps_hbm, decay_hbm, residue_hbm, skip_hbm,
           conv, square, q_ref, k_ref, v_ref, taps_ref, decay_flat, residue_flat, skip_ref,
           tails, halo_out, halo_in, pad, leaving, hrev, entering, mixed, rate, wide_weight,
           total, first_half, carry, carry_in, first_out, first_in, state_out, state_in, square_out, square_in,
           halo_send, halo_recv, state_send, state_recv, square_send, square_recv, load_sem, tail_sem, carry_send, carry_recv):
    tok, channels = q_ref.shape
    half = tok // 2
    tiles = channels // LANES
    PARTS = state_send.shape[0]
    part_tiles = tiles // PARTS
    half_tiles = part_tiles // 2
    per = LANES // modes
    me = lax.axis_index("seq")
    mych = lax.axis_index("ch")
    right, left = lax.rem(me + 1, n), lax.rem(me + n - 1, n)

    def partner(bit):
        return me + bit * (1 - 2 * lax.rem(lax.div(me, bit), 2))

    def scan_copy(p, r):
        return pltpu.make_async_remote_copy(
            state_out.at[p, r] if r else first_out.at[p], state_in.at[p, r] if r else first_in.at[p],
            state_send.at[p, r], state_recv.at[p, r], device_id={"seq": partner(1 << r)}, device_id_type=MESH)

    def share_copy(p):
        return pltpu.make_async_remote_copy(carry.at[p], carry_in.at[p], carry_send.at[p], carry_recv.at[p],
                                            device_id={"seq": partner(1)}, device_id_type=MESH)

    order = ((decay_hbm, decay_flat), (residue_hbm, residue_flat), (k_hbm, k_ref), (v_hbm, v_ref), (taps_hbm, taps_ref),
             (skip_hbm, skip_ref), (q_hbm, q_ref))
    tail_loads = [pltpu.make_async_copy(ref.at[tok - 16:tok, :], tails.at[j], tail_sem.at[j])
                  for j, ref in enumerate((q_hbm, k_hbm, v_hbm))]
    loads = [pltpu.make_async_copy(src, dst, load_sem.at[j]) for j, (src, dst) in enumerate(order)]
    for load in tail_loads + loads:
        load.start()
    barrier = pltpu.get_barrier_semaphore()
    for other in [right, left] + [partner(1 << r) for r in range(rounds)]:
        pl.semaphore_signal(barrier, inc=1, device_id={"seq": other}, device_id_type=MESH)
    for d in range(1, nch):
        pl.semaphore_signal(barrier, inc=1, device_id={"ch": lax.rem(mych + d, nch)}, device_id_type=MESH)

    for load in tail_loads:
        load.wait()

    def make_halo(i, _):
        last = [tails[j, :, tile_at(i)].astype(f32)[14:16] for j in range(3)]
        halo_out[:, tile_at(i)] = jnp.concatenate(last + [jnp.zeros((2, LANES), f32)], axis=0).astype(bf16)
        return 0

    lax.fori_loop(0, tiles, make_halo, 0, unroll=4)
    pl.semaphore_wait(barrier, 2 + rounds + nch - 1)

    halo = pltpu.make_async_remote_copy(halo_out, halo_in, halo_send, halo_recv,
                                        device_id={"seq": right}, device_id_type=MESH)

    @pl.when(me < n - 1)
    def _():
        halo.start()

    lane = lax.broadcasted_iota(jnp.int32, (1, LANES), 1)
    lane_group = lane // modes
    lags_rev = (half - 1 - lax.broadcasted_iota(jnp.int32, (1, half), 1)).astype(f32)
    after = (lax.broadcasted_iota(jnp.int32, (half, 1), 0) + 1).astype(f32)
    own_mode = (lax.broadcasted_iota(jnp.int32, (modes, LANES), 1) % modes
                == lax.broadcasted_iota(jnp.int32, (modes, LANES), 0))

    group_row = lax.broadcasted_iota(jnp.int32, (per, LANES), 0)
    blocks = LANES // per

    def prepare(i, _):
        block = tile_at(lax.div(i, blocks))
        index = jnp.broadcast_to(per * lax.rem(i, blocks) + lane_group, (modes, LANES))
        wide_rate = jnp.take_along_axis(decay_flat[:, block], index, axis=1)
        wide_w = jnp.take_along_axis(residue_flat[:, block], index, axis=1)
        rate[:, tile_at(i)] = wide_rate
        wide_weight[:, tile_at(i)] = wide_w
        powers = []
        for j in range(per):
            col = wide_rate[:, j * modes:j * modes + 1]
            powers.append(jnp.exp2(col * lags_rev).astype(bf16))
        powers = jnp.concatenate(powers, axis=0)
        leaving[tile_at(i), :] = powers
        row = jnp.sum(jnp.where(own_mode, wide_rate, 0.0), axis=0, keepdims=True)
        wrow = jnp.sum(jnp.where(own_mode, wide_w, 0.0), axis=0, keepdims=True)
        spread_w = jnp.where(group_row == lane_group, wrow, 0.0)
        coarse = spread_w.astype(bf16).astype(f32)
        both = jnp.dot(jnp.concatenate([coarse, spread_w - coarse], axis=0).astype(bf16), powers, preferred_element_type=f32)
        hrev[pl.ds(pl.multiple_of(i * per, per), per), :] = both[:per] + both[per:]
        entering[:, tile_at(i)] = jnp.exp2(after * row).astype(bf16)
        return 0

    loads[0].wait()
    loads[1].wait()
    pole = jnp.exp(decay_flat[...])
    residue_flat[...] = residue_flat[...] * jnp.sqrt(1.0 - pole * pole)
    decay_flat[...] = decay_flat[...] * LOG2E
    lax.fori_loop(0, tiles, prepare, 0, unroll=UP)
    for load in loads[2:6]:
        load.wait()

    @pl.when(me > 0)
    def _():
        halo.wait_recv()

    @pl.when(me == 0)
    def _():
        halo_in[...] = jnp.zeros_like(halo_in)

    def short(ref, which, i, slot=0):
        place = 3 * slot + which
        x = ref[:, tile_at(i)].astype(f32)
        pad[place, 8:8 + tok, :] = x
        before = halo_in[:, tile_at(i)].astype(f32)
        pad[place, 0:8, :] = pltpu.roll(before, 6 - 2 * which, 0) if which < 3 else before
        a = [taps_ref[3 * which + t:3 * which + t + 1, tile_at(i)] for t in range(3)]
        return a[0] * x + a[1] * pad[place, 7:7 + tok, :] + a[2] * pad[place, 6:6 + tok, :]

    def pick(stacked):
        out = stacked[0:modes]
        for j in range(1, per):
            out = jnp.where(lane_group == j, stacked[j * modes:(j + 1) * modes], out)
        return out

    def summarize(p):
        def body(i, _):
            pair = [SW * i + u for u in range(SW)]
            values = [(short(k_ref, 1, t, u) * short(v_ref, 2, t, u)).astype(bf16) for u, t in enumerate(pair)]
            for u, t in enumerate(pair):
                mixed[:, tile_at(t)] = values[u]
                sides = jnp.concatenate([values[u][:half], values[u][half:]], axis=1)
                spread = jnp.dot(leaving[tile_at(t), :], sides, preferred_element_type=f32)
                one, two = pick(spread[:, :LANES]), pick(spread[:, LANES:])
                state = jnp.exp2(rate[:, tile_at(t)] * float(half)) * one + two
                first_half[:, tile_at(t)] = one
                total[:, tile_at(t)] = state
                first_out[p, :, tile_at(t - p * part_tiles)] = state.astype(bf16)
            return 0

        lax.fori_loop(p * part_tiles // SW, (p + 1) * part_tiles // SW, body, 0, unroll=SU)

    for p in range(PARTS):
        summarize(p)
        scan_copy(p, 0).start()

    causal = (lax.broadcasted_iota(jnp.int32, (half, LANES), 1)
              <= lax.broadcasted_iota(jnp.int32, (half, LANES), 0))

    def diagonal(state):
        fine = state.astype(bf16).astype(f32)
        return jnp.concatenate([jnp.where(lane_group == j, fine, 0.0) for j in range(per)], axis=0).astype(bf16)

    def convolve_tile(i, slot):
        values = mixed[:, tile_at(i)]
        first, second = values[:half], values[half:]
        sides = jnp.concatenate([first, second], axis=1)
        ent = entering[:, tile_at(i)]
        lines = hrev[pl.ds(pl.multiple_of(i * per, per), per), :]
        left_side, right_side = [], []
        both_groups = jnp.concatenate([lane_group, lane_group], axis=1)
        for j in range(per):
            line = jnp.broadcast_to(lines[j:j + 1], (half, LANES))
            block = pltpu.roll(line, 1, 1, stride=1, stride_axis=0)
            left_side.append(jnp.where(causal, block, 0.0).astype(bf16))
            right_side.append(jnp.where(both_groups == j, sides, jnp.zeros_like(sides)))
        state = diagonal(first_half[:, tile_at(i)] * wide_weight[:, tile_at(i)])
        left_side.append(ent)
        right_side.append(jnp.concatenate([jnp.zeros_like(state), state], axis=1))
        product = jnp.dot(jnp.concatenate(left_side, axis=1), jnp.concatenate(right_side, axis=0),
                          preferred_element_type=f32)
        skip = skip_ref[:, tile_at(i)]
        conv[:half, tile_at(i)] = product[:, :LANES] + skip * first.astype(f32)
        conv[half:, tile_at(i)] = product[:, LANES:] + skip * second.astype(f32)
        q_ref[:, tile_at(i)] = short(q_ref, 0, i, slot).astype(bf16)

    def convolve(i, _):
        for u in range(CW):
            convolve_tile(CW * i + u, u)
        return 0

    loads[6].wait()

    carry[...] = jnp.zeros_like(carry)
    core = lax.rem(me, 2)
    steps = tiles // CW
    lead = min(LEAD, steps)
    shares = [2] * (rounds - 2) + [LASTW]
    bounds = [0] + [lead + (steps - lead) * sum(shares[:r]) // sum(shares) for r in range(rounds)]
    for r in range(rounds):
        bit = 1 << r
        last = r == rounds - 1
        upper = lax.rem(lax.div(me, bit), 2) == 1
        lax.fori_loop(bounds[r], bounds[r + 1], convolve, 0, unroll=CU)
        block_rate = float(tok * bit)
        offset = ((lax.rem(me, bit) - core) * tok).astype(f32) if r else None

        def merge(p, i):
            local = core * half_tiles + i
            place = tile_at(p * part_tiles + local)
            theirs = (state_in[p, r, :, tile_at(i)] if r else first_in[p, :, tile_at(local)]).astype(f32)
            logs = rate[:, place]
            if r:
                inward = jnp.exp2(logs * offset) * theirs
                carry[p, :, tile_at(i)] += jnp.where(upper, inward, 0.0)
            if not last:
                mine = total[:, place]
                later = jnp.where(upper, mine, theirs)
                before = jnp.where(upper, theirs, mine)
                both = jnp.exp2(logs * block_rate) * before + later
                total[:, place] = both
                state_out[p, r + 1, :, tile_at(i)] = both.astype(bf16)

        def arrive(p):
            scan_copy(p, r).wait_recv()

            def body(i, _):
                merge(p, i)
                return 0

            lax.fori_loop(0, half_tiles, body, 0, unroll=4)

        for p in range(PARTS):
            if last:
                @pl.when(upper)
                def _():
                    arrive(p)

                share_copy(p).start()
            else:
                arrive(p)
                following = scan_copy(p, r + 1)
                if r + 1 == rounds - 1:
                    @pl.when(lax.rem(lax.div(me, 2 * bit), 2) == 0)
                    def _():
                        following.start()
                else:
                    following.start()

    def assemble(p):
        def body(i, _):
            for part, side in ((carry, core), (carry_in, 1 - core)):
                local = side * half_tiles + i
                place = tile_at(p * part_tiles + local)
                entry = part[p, :, tile_at(i)]
                moved = jnp.exp2(rate[:, place] * float(tok)) * entry + first_in[p, :, tile_at(local)].astype(f32)
                total[:, place] = jnp.where(core == 1, moved, entry)
            return 0

        lax.fori_loop(0, half_tiles, body, 0, unroll=2)

    square[...] = jnp.zeros_like(square)

    def gated_tile(i):
        state = total[:, tile_at(i)] * wide_weight[:, tile_at(i)]
        later = state * jnp.exp2(rate[:, tile_at(i)] * float(half))
        columns = []
        for s in (state, later):
            fine = s.astype(bf16).astype(f32)
            columns.append(jnp.concatenate([diagonal(fine), diagonal(s - fine)], axis=0))
        ent = entering[:, tile_at(i)]
        carried = jnp.dot(jnp.concatenate([ent, ent], axis=1), jnp.concatenate(columns, axis=1),
                          preferred_element_type=f32)
        gated = []
        for side in range(2):
            rows = slice(side * half, (side + 1) * half)
            g = q_ref[rows, tile_at(i)].astype(f32) * (conv[rows, tile_at(i)] + carried[:, side * LANES:(side + 1) * LANES])
            conv[rows, tile_at(i)] = g
            gated.append(g)
        return gated

    def gate(i, _):
        done = [gated_tile(GW * i + u) for u in range(GW)]
        for side in range(2):
            rows = slice(side * half, (side + 1) * half)
            square[rows, :] += sum(g[side] * g[side] for g in done)
        return 0

    for p in range(PARTS):
        share_copy(p).wait()
        assemble(p)
        lax.fori_loop(p * part_tiles // GW, (p + 1) * part_tiles // GW, gate, 0, unroll=GU)

    sums = jnp.sum(square[...].T, axis=0, keepdims=True)
    square_out[...] = jnp.broadcast_to(sums, square_out.shape)
    copies = []
    for d in range(1, nch):
        c = pltpu.make_async_remote_copy(square_out, square_in.at[d - 1], square_send.at[d - 1], square_recv.at[d - 1],
                                         device_id={"ch": lax.rem(mych + d, nch)}, device_id_type=MESH)
        c.start()
        copies.append(c)
    for d, c in enumerate(copies):
        c.wait()
        sums = sums + square_in[d, 0:1, :]
    scale = lax.rsqrt(sums / (channels * nch) + 1e-5)
    square[...] = jnp.broadcast_to(scale, (LANES, tok)).T

    @pl.when(me < n - 1)
    def _():
        halo.wait_send()

    for p in range(PARTS):
        for r in range(rounds):
            bit = 1 << r
            copy = scan_copy(p, r)
            if r == rounds - 1:
                @pl.when(lax.rem(lax.div(me, bit), 2) == 0)
                def _():
                    copy.wait_send()
            else:
                copy.wait_send()


def normalize(gated_ref, scale_ref, gain_ref, out_hbm, out_ref, sem):
    pieces = out_ref.shape[0]
    width = out_ref.shape[2]

    def copy(j):
        return pltpu.make_async_copy(out_ref.at[j], out_hbm.at[:, j * width:(j + 1) * width], sem.at[j])

    for j in range(pieces):
        for i in range(width // LANES):
            place = slice(j * width + i * LANES, j * width + (i + 1) * LANES)
            out_ref[j, :, i * LANES:(i + 1) * LANES] = (gated_ref[:, place] * scale_ref[...] * gain_ref[:, place]).astype(bf16)
        copy(j).start()
    for j in range(pieces):
        copy(j).wait()


def on_device(n, nch, q_proj, k_proj, v_proj, short_filter, log_decay, residue, skip_bias, norm_gain):
    tok, channels = q_proj.shape
    groups, modes = log_decay.shape
    rounds = n.bit_length() - 1
    assert channels % (4 * LANES) == 0 and n == 1 << rounds and rounds > 1 and channels == groups * modes
    vmem = pl.BlockSpec(memory_space=pltpu.VMEM)
    dma = pltpu.SemaphoreType.DMA
    PARTS = min(MOST_PARTS, channels // (4 * LANES))
    part = channels // PARTS
    gated, scale = pl.pallas_call(
        functools.partial(kernel, n, nch, rounds, modes),
        out_shape=(jax.ShapeDtypeStruct((tok, channels), f32), jax.ShapeDtypeStruct((tok, LANES), f32)),
        in_specs=[pl.BlockSpec(memory_space=pltpu.HBM)] * 7,
        out_specs=(vmem, vmem),
        scratch_shapes=[
            pltpu.VMEM((tok, channels), bf16),
            pltpu.VMEM((tok, channels), bf16),
            pltpu.VMEM((tok, channels), bf16),
            pltpu.VMEM((9, channels), f32),
            pltpu.VMEM((modes, groups), f32),
            pltpu.VMEM((modes, groups), f32),
            pltpu.VMEM((1, channels), f32),
            pltpu.VMEM((3, 16, channels), bf16),
            pltpu.VMEM((8, channels), bf16),
            pltpu.VMEM((8, channels), bf16),
            pltpu.VMEM((3 * max(SW, CW), tok + 8, LANES), f32),
            pltpu.VMEM((channels, tok // 2), bf16),
            pltpu.VMEM((groups, tok // 2), f32),
            pltpu.VMEM((tok // 2, channels), bf16),
            pltpu.VMEM((tok, channels), bf16),
            pltpu.VMEM((modes, channels), f32),
            pltpu.VMEM((modes, channels), f32),
            pltpu.VMEM((modes, channels), f32),
            pltpu.VMEM((modes, channels), f32),
            pltpu.VMEM((PARTS, modes, part // 2), f32),
            pltpu.VMEM((PARTS, modes, part // 2), f32),
            pltpu.VMEM((PARTS, modes, part), bf16),
            pltpu.VMEM((PARTS, modes, part), bf16),
            pltpu.VMEM((PARTS, rounds, modes, part // 2), bf16),
            pltpu.VMEM((PARTS, rounds, modes, part // 2), bf16),
            pltpu.VMEM((8, tok), f32),
            pltpu.VMEM((max(nch - 1, 1), 8, tok), f32),
            dma, dma, dma((PARTS, rounds)), dma((PARTS, rounds)), dma((max(nch - 1, 1),)), dma((max(nch - 1, 1),)),
            dma((7,)), dma((3,)), dma((PARTS,)), dma((PARTS,)),
        ],
        compiler_params=pltpu.CompilerParams(collective_id=0, has_side_effects=True,
                                             vmem_limit_bytes=LIMIT_A),
    )(*[pltpu.with_memory_space_constraint(x, pltpu.HBM) for x in (q_proj, k_proj, v_proj, short_filter, log_decay.T, residue.T, skip_bias.reshape(1, channels))])
    pieces = 8
    return pl.pallas_call(
        normalize,
        out_shape=jax.ShapeDtypeStruct((tok, channels), bf16),
        in_specs=[vmem, vmem, vmem],
        out_specs=pl.BlockSpec(memory_space=pltpu.HBM),
        scratch_shapes=[pltpu.VMEM((pieces, tok, channels // pieces), bf16), dma((pieces,))],
        compiler_params=pltpu.CompilerParams(vmem_limit_bytes=LIMIT_B),
    )(gated, scale, norm_gain.reshape(1, channels))


UP = 8
SW, SU, CW, CU, GW, GU, LEAD, LASTW = 2, 4, 2, 2, 2, 4, 1, 2
LIMIT_A = 28 * 1024 * 1024
LIMIT_B = 16 * 1024 * 1024


def solution(mesh):
    return jax.shard_map(
        functools.partial(on_device, mesh.shape["seq"], mesh.shape["ch"]),
        mesh=mesh,
        in_specs=(P("seq", "ch"), P("seq", "ch"), P("seq", "ch"), P(None, "ch"),
                  P("ch", None), P("ch", None), P("ch"), P("ch")),
        out_specs=P("seq", "ch"),
        check_vma=False,
    )
```

```python
import functools
import jax
import jax.numpy as jnp
from jax import lax
from jax.experimental import pallas as pl
from jax.experimental.pallas import tpu as pltpu
from jax.sharding import PartitionSpec as P

LANES = 128
MOST_PARTS = 4
MESH = pl.DeviceIdType.MESH
f32 = jnp.float32
LOG2E = 1.4426950408889634
bf16 = jnp.bfloat16


def tile_at(i):
    return pl.ds(pl.multiple_of(i * LANES, LANES), LANES)


def kernel(n, nch, rounds, modes, q_hbm, k_hbm, v_hbm, taps_hbm, decay_hbm, residue_hbm, skip_hbm,
           conv, square, q_ref, k_ref, v_ref, taps_ref, decay_flat, residue_flat, skip_ref,
           tails, halo_out, halo_in, pad, leaving, hrev, entering, mixed, q_short, rate, wide_weight,
           total, first_half, carry, carry_in, first_out, first_in, state_out, state_in, square_out, square_in,
           halo_send, halo_recv, state_send, state_recv, square_send, square_recv, load_sem, tail_sem, carry_send, carry_recv):
    tok, channels = q_ref.shape
    half = tok // 2
    tiles = channels // LANES
    PARTS = state_send.shape[0]
    part_tiles = tiles // PARTS
    half_tiles = part_tiles // 2
    per = LANES // modes
    me = lax.axis_index("seq")
    mych = lax.axis_index("ch")
    right = lax.rem(me + 1, n)

    def partner(bit):
        return me + bit * (1 - 2 * lax.rem(lax.div(me, bit), 2))

    def scan_copy(p, r):
        return pltpu.make_async_remote_copy(
            state_out.at[p, r] if r else first_out.at[p], state_in.at[p, r] if r else first_in.at[p],
            state_send.at[p, r], state_recv.at[p, r], device_id={"seq": partner(1 << r)}, device_id_type=MESH)

    def share_copy(p):
        return pltpu.make_async_remote_copy(carry.at[p], carry_in.at[p], carry_send.at[p], carry_recv.at[p],
                                            device_id={"seq": partner(1)}, device_id_type=MESH)

    order = ((decay_hbm, decay_flat), (residue_hbm, residue_flat), (k_hbm, k_ref), (v_hbm, v_ref), (taps_hbm, taps_ref),
             (skip_hbm, skip_ref), (q_hbm, q_ref))
    tail_loads = [pltpu.make_async_copy(ref.at[tok - 16:tok, :], tails.at[j], tail_sem.at[j])
                  for j, ref in enumerate((q_hbm, k_hbm, v_hbm))]
    loads = [pltpu.make_async_copy(src, dst, load_sem.at[j]) for j, (src, dst) in enumerate(order)]
    for load in tail_loads + loads:
        load.start()
    barrier = pltpu.get_barrier_semaphore()
    top = n // 2

    def ready(device):
        pl.semaphore_signal(barrier, inc=1, device_id=device, device_id_type=MESH)

    @pl.when(me >= top)
    def _():
        ready({"seq": me - top})

    @pl.when(me > 0)
    def _():
        ready({"seq": me - 1})

    for r in range(rounds - 1):
        ready({"seq": partner(1 << r)})
    for d in range(1, nch):
        ready({"ch": lax.rem(mych + d, nch)})

    for load in tail_loads:
        load.wait()

    def make_halo(i, _):
        last = [tails[j, :, tile_at(i)].astype(f32)[14:16] for j in range(3)]
        halo_out[:, tile_at(i)] = jnp.concatenate(last + [jnp.zeros((2, LANES), f32)], axis=0).astype(bf16)
        return 0

    lax.fori_loop(0, tiles, make_halo, 0, unroll=4)
    fixed = rounds - 1 + nch - 1
    pl.semaphore_wait(barrier, fixed + (me < n - 1).astype(jnp.int32) + (me < top).astype(jnp.int32))

    halo = pltpu.make_async_remote_copy(halo_out, halo_in, halo_send, halo_recv,
                                        device_id={"seq": right}, device_id_type=MESH)

    @pl.when(me < n - 1)
    def _():
        halo.start()

    lane = lax.broadcasted_iota(jnp.int32, (1, LANES), 1)
    lane_group = lane // modes
    lags_rev = (half - 1 - lax.broadcasted_iota(jnp.int32, (1, half), 1)).astype(f32)
    after = (lax.broadcasted_iota(jnp.int32, (half, 1), 0) + 1).astype(f32)
    own_mode = (lax.broadcasted_iota(jnp.int32, (modes, LANES), 1) % modes
                == lax.broadcasted_iota(jnp.int32, (modes, LANES), 0))

    group_row = lax.broadcasted_iota(jnp.int32, (per, LANES), 0)
    blocks = LANES // per

    def prepare(i, _):
        block = tile_at(lax.div(i, blocks))
        index = jnp.broadcast_to(per * lax.rem(i, blocks) + lane_group, (modes, LANES))
        wide_rate = jnp.take_along_axis(decay_flat[:, block], index, axis=1)
        wide_w = jnp.take_along_axis(residue_flat[:, block], index, axis=1)
        rate[:, tile_at(i)] = wide_rate
        wide_weight[:, tile_at(i)] = wide_w
        powers = []
        for j in range(per):
            col = wide_rate[:, j * modes:j * modes + 1]
            powers.append(jnp.exp2(col * lags_rev).astype(bf16))
        powers = jnp.concatenate(powers, axis=0)
        leaving[tile_at(i), :] = powers
        row = jnp.sum(jnp.where(own_mode, wide_rate, 0.0), axis=0, keepdims=True)
        wrow = jnp.sum(jnp.where(own_mode, wide_w, 0.0), axis=0, keepdims=True)
        spread_w = jnp.where(group_row == lane_group, wrow, 0.0)
        coarse = spread_w.astype(bf16).astype(f32)
        both = jnp.dot(jnp.concatenate([coarse, spread_w - coarse], axis=0).astype(bf16), powers, preferred_element_type=f32)
        hrev[pl.ds(pl.multiple_of(i * per, per), per), :] = both[:per] + both[per:]
        entering[i] = jnp.exp2(after * row).astype(bf16)
        return 0

    loads[0].wait()
    loads[1].wait()
    pole = jnp.exp(decay_flat[...])
    residue_flat[...] = residue_flat[...] * jnp.sqrt(1.0 - pole * pole)
    decay_flat[...] = decay_flat[...] * LOG2E
    lax.fori_loop(0, tiles, prepare, 0, unroll=UP)
    for load in loads[2:6]:
        load.wait()

    @pl.when(me > 0)
    def _():
        halo.wait_recv()

    @pl.when(me == 0)
    def _():
        halo_in[...] = jnp.zeros_like(halo_in)

    def short(ref, which, i, slot=0):
        place = 3 * slot + which
        x = ref[:, tile_at(i)].astype(f32)
        pad[place, 8:8 + tok, :] = x
        before = halo_in[:, tile_at(i)].astype(f32)
        pad[place, 0:8, :] = pltpu.roll(before, 6 - 2 * which, 0) if which < 3 else before
        a = [taps_ref[3 * which + t:3 * which + t + 1, tile_at(i)] for t in range(3)]
        return a[0] * x + a[1] * pad[place, 7:7 + tok, :] + a[2] * pad[place, 6:6 + tok, :]

    def pick(stacked):
        out = stacked[0:modes]
        for j in range(1, per):
            out = jnp.where(lane_group == j, stacked[j * modes:(j + 1) * modes], out)
        return out

    def summarize(p):
        def body(i, _):
            pair = [SW * i + u for u in range(SW)]
            values = [(short(k_ref, 1, t, u) * short(v_ref, 2, t, u)).astype(bf16) for u, t in enumerate(pair)]
            for u, t in enumerate(pair):
                mixed[t] = values[u]
                sides = jnp.concatenate([values[u][:half], values[u][half:]], axis=1)
                spread = jnp.dot(leaving[tile_at(t), :], sides, preferred_element_type=f32)
                one, two = pick(spread[:, :LANES]), pick(spread[:, LANES:])
                state = jnp.exp2(rate[:, tile_at(t)] * float(half)) * one + two
                first_half[:, tile_at(t)] = one
                total[:, tile_at(t)] = state
                first_out[p, :, tile_at(t - p * part_tiles)] = state.astype(bf16)
            return 0

        lax.fori_loop(p * part_tiles // SW, (p + 1) * part_tiles // SW, body, 0, unroll=SU)

    causal = (lax.broadcasted_iota(jnp.int32, (half, LANES), 1)
              <= lax.broadcasted_iota(jnp.int32, (half, LANES), 0))

    def diagonal(state):
        fine = state.astype(bf16).astype(f32)
        return jnp.concatenate([jnp.where(lane_group == j, fine, 0.0) for j in range(per)], axis=0).astype(bf16)

    def convolve_tile(i, slot):
        values = mixed[i]
        first, second = values[:half], values[half:]
        sides = jnp.concatenate([first, second], axis=1)
        ent = entering[i]
        lines = hrev[pl.ds(pl.multiple_of(i * per, per), per), :]
        left_side, right_side = [], []
        both_groups = jnp.concatenate([lane_group, lane_group], axis=1)
        for j in range(per):
            line = jnp.broadcast_to(lines[j:j + 1], (half, LANES))
            block = pltpu.roll(line, 1, 1, stride=1, stride_axis=0)
            left_side.append(jnp.where(causal, block, 0.0).astype(bf16))
            right_side.append(jnp.where(both_groups == j, sides, jnp.zeros_like(sides)))
        state = diagonal(first_half[:, tile_at(i)] * wide_weight[:, tile_at(i)])
        left_side.append(ent)
        right_side.append(jnp.concatenate([jnp.zeros_like(state), state], axis=1))
        product = jnp.dot(jnp.concatenate(left_side, axis=1), jnp.concatenate(right_side, axis=0),
                          preferred_element_type=f32)
        skip = skip_ref[:, tile_at(i)]
        conv[:half, tile_at(i)] = product[:, :LANES] + skip * first.astype(f32)
        conv[half:, tile_at(i)] = product[:, LANES:] + skip * second.astype(f32)
        q_short[i] = short(q_ref, 0, i, slot).astype(bf16)

    def convolve(i, _):
        for u in range(CW):
            convolve_tile(CW * i + u, u)
        return 0

    carry[...] = jnp.zeros_like(carry)
    core = lax.rem(me, 2)

    def arrive(p, r):
        bit = 1 << r
        last = r == rounds - 1
        upper = lax.rem(lax.div(me, bit), 2) == 1
        block_rate = float(tok * bit)
        offset = ((lax.rem(me, bit) - core) * tok).astype(f32) if r else None

        def merge(i, _):
            local = core * half_tiles + i
            place = tile_at(p * part_tiles + local)
            theirs = (state_in[p, r, :, tile_at(i)] if r else first_in[p, :, tile_at(local)]).astype(f32)
            logs = rate[:, place]
            if r:
                inward = jnp.exp2(logs * offset) * theirs
                carry[p, :, tile_at(i)] += jnp.where(upper, inward, 0.0)
            if not last:
                mine = total[:, place]
                later = jnp.where(upper, mine, theirs)
                before = jnp.where(upper, theirs, mine)
                both = jnp.exp2(logs * block_rate) * before + later
                total[:, place] = both
                state_out[p, r + 1, :, tile_at(i)] = both.astype(bf16)
            return 0

        def receive():
            scan_copy(p, r).wait_recv()
            lax.fori_loop(0, half_tiles, merge, 0, unroll=4)

        if last:
            pl.when(upper)(receive)
            share_copy(p).start()
        else:
            receive()
            following = scan_copy(p, r + 1)
            if r + 1 == rounds - 1:
                pl.when(lax.rem(lax.div(me, 2 * bit), 2) == 0)(following.start)
            else:
                following.start()

    for p in range(PARTS):
        summarize(p)
        scan_copy(p, 0).start()
        if p:
            arrive(p - 1, 0)

    loads[6].wait()
    events = [(PARTS - 1, 0)] + [(p, r) for r in range(1, rounds) for p in range(PARTS)]
    shares = [LEAD] + [FIRST if p == 0 else THEN for r in range(1, rounds) for p in range(PARTS)]
    steps = tiles // CW
    done = 0
    for k, (p, r) in enumerate(events):
        end = (steps * sum(shares[:k + 1]) + sum(shares) // 2) // sum(shares)
        if end > done:
            lax.fori_loop(done, end, convolve, 0, unroll=CU)
        done = end
        arrive(p, r)

    def assemble(p):
        def body(i, _):
            for part, side in ((carry, core), (carry_in, 1 - core)):
                local = side * half_tiles + i
                place = tile_at(p * part_tiles + local)
                entry = part[p, :, tile_at(i)]
                moved = jnp.exp2(rate[:, place] * float(tok)) * entry + first_in[p, :, tile_at(local)].astype(f32)
                total[:, place] = jnp.where(core == 1, moved, entry)
            return 0

        lax.fori_loop(0, half_tiles, body, 0, unroll=2)

    square[...] = jnp.zeros_like(square)

    def gated_tile(i):
        state = total[:, tile_at(i)] * wide_weight[:, tile_at(i)]
        later = state * jnp.exp2(rate[:, tile_at(i)] * float(half))
        columns = []
        for s in (state, later):
            fine = s.astype(bf16).astype(f32)
            columns.append(jnp.concatenate([diagonal(fine), diagonal(s - fine)], axis=0))
        ent = entering[i]
        carried = jnp.dot(jnp.concatenate([ent, ent], axis=1), jnp.concatenate(columns, axis=1),
                          preferred_element_type=f32)
        gated = []
        for side in range(2):
            rows = slice(side * half, (side + 1) * half)
            g = q_short[i, rows, :].astype(f32) * (conv[rows, tile_at(i)] + carried[:, side * LANES:(side + 1) * LANES])
            conv[rows, tile_at(i)] = g
            gated.append(g)
        return gated

    def gate(i, _):
        done = [gated_tile(GW * i + u) for u in range(GW)]
        for side in range(2):
            rows = slice(side * half, (side + 1) * half)
            square[rows, :] += sum(g[side] * g[side] for g in done)
        return 0

    for p in range(PARTS):
        share_copy(p).wait()
        assemble(p)
        lax.fori_loop(p * part_tiles // GW, (p + 1) * part_tiles // GW, gate, 0, unroll=GU)

    sums = jnp.sum(square[...].T, axis=0, keepdims=True)
    square_out[...] = jnp.broadcast_to(sums, square_out.shape)
    copies = []
    for d in range(1, nch):
        c = pltpu.make_async_remote_copy(square_out, square_in.at[d - 1], square_send.at[d - 1], square_recv.at[d - 1],
                                         device_id={"ch": lax.rem(mych + d, nch)}, device_id_type=MESH)
        c.start()
        copies.append(c)
    for d, c in enumerate(copies):
        c.wait()
        sums = sums + square_in[d, 0:1, :]
    scale = lax.rsqrt(sums / (channels * nch) + 1e-5)
    square[...] = jnp.broadcast_to(scale, (LANES, tok)).T

    @pl.when(me < n - 1)
    def _():
        halo.wait_send()

    for p in range(PARTS):
        for r in range(rounds):
            bit = 1 << r
            copy = scan_copy(p, r)
            if r == rounds - 1:
                @pl.when(lax.rem(lax.div(me, bit), 2) == 0)
                def _():
                    copy.wait_send()
            else:
                copy.wait_send()


def normalize(gated_ref, scale_ref, gain_ref, out_hbm, out_ref, sem):
    pieces = out_ref.shape[0]
    width = out_ref.shape[2]

    def copy(j):
        return pltpu.make_async_copy(out_ref.at[j], out_hbm.at[:, j * width:(j + 1) * width], sem.at[j])

    for j in range(pieces):
        for i in range(width // LANES):
            place = slice(j * width + i * LANES, j * width + (i + 1) * LANES)
            out_ref[j, :, i * LANES:(i + 1) * LANES] = (gated_ref[:, place] * scale_ref[...] * gain_ref[:, place]).astype(bf16)
        copy(j).start()
    for j in range(pieces):
        copy(j).wait()


def on_device(n, nch, q_proj, k_proj, v_proj, short_filter, log_decay, residue, skip_bias, norm_gain):
    tok, channels = q_proj.shape
    groups, modes = log_decay.shape
    rounds = n.bit_length() - 1
    assert channels % (4 * LANES) == 0 and n == 1 << rounds and rounds > 1 and channels == groups * modes
    vmem = pl.BlockSpec(memory_space=pltpu.VMEM)
    dma = pltpu.SemaphoreType.DMA
    PARTS = min(MOST_PARTS, channels // (4 * LANES))
    part = channels // PARTS
    gated, scale = pl.pallas_call(
        functools.partial(kernel, n, nch, rounds, modes),
        out_shape=(jax.ShapeDtypeStruct((tok, channels), f32), jax.ShapeDtypeStruct((tok, LANES), f32)),
        in_specs=[pl.BlockSpec(memory_space=pltpu.HBM)] * 7,
        out_specs=(vmem, vmem),
        scratch_shapes=[
            pltpu.VMEM((tok, channels), bf16),
            pltpu.VMEM((tok, channels), bf16),
            pltpu.VMEM((tok, channels), bf16),
            pltpu.VMEM((9, channels), f32),
            pltpu.VMEM((modes, groups), f32),
            pltpu.VMEM((modes, groups), f32),
            pltpu.VMEM((1, channels), f32),
            pltpu.VMEM((3, 16, channels), bf16),
            pltpu.VMEM((8, channels), bf16),
            pltpu.VMEM((8, channels), bf16),
            pltpu.VMEM((3 * max(SW, CW), tok + 8, LANES), f32),
            pltpu.VMEM((channels, tok // 2), bf16),
            pltpu.VMEM((groups, tok // 2), f32),
            pltpu.VMEM((channels // LANES, tok // 2, LANES), bf16),
            pltpu.VMEM((channels // LANES, tok, LANES), bf16),
            pltpu.VMEM((channels // LANES, tok, LANES), bf16),
            pltpu.VMEM((modes, channels), f32),
            pltpu.VMEM((modes, channels), f32),
            pltpu.VMEM((modes, channels), f32),
            pltpu.VMEM((modes, channels), f32),
            pltpu.VMEM((PARTS, modes, part // 2), f32),
            pltpu.VMEM((PARTS, modes, part // 2), f32),
            pltpu.VMEM((PARTS, modes, part), bf16),
            pltpu.VMEM((PARTS, modes, part), bf16),
            pltpu.VMEM((PARTS, rounds, modes, part // 2), bf16),
            pltpu.VMEM((PARTS, rounds, modes, part // 2), bf16),
            pltpu.VMEM((8, tok), f32),
            pltpu.VMEM((max(nch - 1, 1), 8, tok), f32),
            dma, dma, dma((PARTS, rounds)), dma((PARTS, rounds)), dma((max(nch - 1, 1),)), dma((max(nch - 1, 1),)),
            dma((7,)), dma((3,)), dma((PARTS,)), dma((PARTS,)),
        ],
        compiler_params=pltpu.CompilerParams(collective_id=0, has_side_effects=True,
                                             vmem_limit_bytes=LIMIT_A),
    )(*[pltpu.with_memory_space_constraint(x, pltpu.HBM) for x in (q_proj, k_proj, v_proj, short_filter, log_decay.T, residue.T, skip_bias.reshape(1, channels))])
    pieces = 8
    return pl.pallas_call(
        normalize,
        out_shape=jax.ShapeDtypeStruct((tok, channels), bf16),
        in_specs=[vmem, vmem, vmem],
        out_specs=pl.BlockSpec(memory_space=pltpu.HBM),
        scratch_shapes=[pltpu.VMEM((pieces, tok, channels // pieces), bf16), dma((pieces,))],
        compiler_params=pltpu.CompilerParams(vmem_limit_bytes=LIMIT_B),
    )(gated, scale, norm_gain.reshape(1, channels))


UP = 8
SW, SU, CW, CU, GW, GU, LEAD, FIRST, THEN = 2, 4, 2, 2, 2, 4, 2, 5, 2
LIMIT_A = 28 * 1024 * 1024
LIMIT_B = 16 * 1024 * 1024


def solution(mesh):
    return jax.shard_map(
        functools.partial(on_device, mesh.shape["seq"], mesh.shape["ch"]),
        mesh=mesh,
        in_specs=(P("seq", "ch"), P("seq", "ch"), P("seq", "ch"), P(None, "ch"),
                  P("ch", None), P("ch", None), P("ch"), P("ch")),
        out_specs=P("seq", "ch"),
        check_vma=False,
    )
```

```python
import functools
import jax
import jax.numpy as jnp
from jax import lax
from jax.experimental import pallas as pl
from jax.experimental.pallas import tpu as pltpu
from jax.sharding import PartitionSpec as P

LANES = 128
MOST_PARTS = 4
MESH = pl.DeviceIdType.MESH
f32 = jnp.float32
LOG2E = 1.4426950408889634
bf16 = jnp.bfloat16


def tile_at(i):
    return pl.ds(pl.multiple_of(i * LANES, LANES), LANES)


def kernel(n, nch, rounds, modes, q_hbm, k_hbm, v_hbm, taps_hbm, decay_hbm, residue_hbm, skip_hbm,
           conv, square, q_ref, k_ref, v_ref, taps_ref, decay_flat, residue_flat, skip_ref,
           tails, halo_out, halo_in, pad, leaving, hrev, entering, mixed, q_short, rate, wide_weight,
           total, first_half, carry, carry_in, first_out, first_in, state_out, state_in, square_out, square_in,
           halo_send, halo_recv, state_send, state_recv, square_send, square_recv, load_sem, tail_sem, carry_send, carry_recv):
    tok, channels = q_ref.shape
    half = tok // 2
    tiles = channels // LANES
    PARTS = state_send.shape[0]
    part_tiles = tiles // PARTS
    half_tiles = part_tiles // 2
    per = LANES // modes
    me = lax.axis_index("seq")
    mych = lax.axis_index("ch")
    right = lax.rem(me + 1, n)

    def partner(bit):
        return me + bit * (1 - 2 * lax.rem(lax.div(me, bit), 2))

    def scan_copy(p, r):
        return pltpu.make_async_remote_copy(
            state_out.at[p, r] if r else first_out.at[p], state_in.at[p, r] if r else first_in.at[p],
            state_send.at[p, r], state_recv.at[p, r], device_id={"seq": partner(1 << r)}, device_id_type=MESH)

    def share_copy(p):
        return pltpu.make_async_remote_copy(carry.at[p], carry_in.at[p], carry_send.at[p], carry_recv.at[p],
                                            device_id={"seq": partner(1)}, device_id_type=MESH)

    order = ((decay_hbm, decay_flat), (residue_hbm, residue_flat), (k_hbm, k_ref), (v_hbm, v_ref), (taps_hbm, taps_ref),
             (skip_hbm, skip_ref), (q_hbm, q_ref))
    tail_loads = [pltpu.make_async_copy(ref.at[tok - 16:tok, :], tails.at[j], tail_sem.at[j])
                  for j, ref in enumerate((q_hbm, k_hbm, v_hbm))]
    loads = [pltpu.make_async_copy(src, dst, load_sem.at[j]) for j, (src, dst) in enumerate(order)]
    for load in tail_loads + loads:
        load.start()
    barrier = pltpu.get_barrier_semaphore()
    top = n // 2

    def ready(device):
        pl.semaphore_signal(barrier, inc=1, device_id=device, device_id_type=MESH)

    @pl.when(me >= top)
    def _():
        ready({"seq": me - top})

    @pl.when(me > 0)
    def _():
        ready({"seq": me - 1})

    for r in range(rounds - 1):
        ready({"seq": partner(1 << r)})
    for d in range(1, nch):
        ready({"ch": lax.rem(mych + d, nch)})

    for load in tail_loads:
        load.wait()

    def make_halo(i, _):
        last = [tails[j, :, tile_at(i)].astype(f32)[14:16] for j in range(3)]
        halo_out[:, tile_at(i)] = jnp.concatenate(last + [jnp.zeros((2, LANES), f32)], axis=0).astype(bf16)
        return 0

    lax.fori_loop(0, tiles, make_halo, 0, unroll=4)
    fixed = rounds - 1 + nch - 1
    pl.semaphore_wait(barrier, fixed + (me < n - 1).astype(jnp.int32) + (me < top).astype(jnp.int32))

    halo = pltpu.make_async_remote_copy(halo_out, halo_in, halo_send, halo_recv,
                                        device_id={"seq": right}, device_id_type=MESH)

    @pl.when(me < n - 1)
    def _():
        halo.start()

    lane = lax.broadcasted_iota(jnp.int32, (1, LANES), 1)
    lane_group = lane // modes
    lags_rev = (half - 1 - lax.broadcasted_iota(jnp.int32, (1, half), 1)).astype(f32)
    after = (lax.broadcasted_iota(jnp.int32, (half, 1), 0) + 1).astype(f32)
    own_mode = (lax.broadcasted_iota(jnp.int32, (modes, LANES), 1) % modes
                == lax.broadcasted_iota(jnp.int32, (modes, LANES), 0))

    group_row = lax.broadcasted_iota(jnp.int32, (per, LANES), 0)
    blocks = LANES // per

    def prepare(i, _):
        block = tile_at(lax.div(i, blocks))
        index = jnp.broadcast_to(per * lax.rem(i, blocks) + lane_group, (modes, LANES))
        wide_rate = jnp.take_along_axis(decay_flat[:, block], index, axis=1)
        wide_w = jnp.take_along_axis(residue_flat[:, block], index, axis=1)
        rate[:, tile_at(i)] = wide_rate
        wide_weight[:, tile_at(i)] = wide_w
        powers = []
        for j in range(per):
            col = wide_rate[:, j * modes:j * modes + 1]
            powers.append(jnp.exp2(col * lags_rev).astype(bf16))
        powers = jnp.concatenate(powers, axis=0)
        leaving[tile_at(i), :] = powers
        row = jnp.sum(jnp.where(own_mode, wide_rate, 0.0), axis=0, keepdims=True)
        wrow = jnp.sum(jnp.where(own_mode, wide_w, 0.0), axis=0, keepdims=True)
        spread_w = jnp.where(group_row == lane_group, wrow, 0.0)
        coarse = spread_w.astype(bf16).astype(f32)
        both = jnp.dot(jnp.concatenate([coarse, spread_w - coarse], axis=0).astype(bf16), powers, preferred_element_type=f32)
        hrev[pl.ds(pl.multiple_of(i * per, per), per), :] = both[:per] + both[per:]
        entering[i] = jnp.exp2(after * row).astype(bf16)
        return 0

    loads[0].wait()
    loads[1].wait()
    pole = jnp.exp(decay_flat[...])
    residue_flat[...] = residue_flat[...] * jnp.sqrt(1.0 - pole * pole)
    decay_flat[...] = decay_flat[...] * LOG2E
    lax.fori_loop(0, tiles, prepare, 0, unroll=UP)
    for load in loads[2:6]:
        load.wait()

    @pl.when(me > 0)
    def _():
        halo.wait_recv()

    @pl.when(me == 0)
    def _():
        halo_in[...] = jnp.zeros_like(halo_in)

    def short(ref, which, i, slot=0):
        place = 3 * slot + which
        x = ref[:, tile_at(i)].astype(f32)
        pad[place, 8:8 + tok, :] = x
        before = halo_in[:, tile_at(i)].astype(f32)
        pad[place, 0:8, :] = pltpu.roll(before, 6 - 2 * which, 0) if which < 3 else before
        a = [taps_ref[3 * which + t:3 * which + t + 1, tile_at(i)] for t in range(3)]
        return a[0] * x + a[1] * pad[place, 7:7 + tok, :] + a[2] * pad[place, 6:6 + tok, :]

    def pick(stacked):
        out = stacked[0:modes]
        for j in range(1, per):
            out = jnp.where(lane_group == j, stacked[j * modes:(j + 1) * modes], out)
        return out

    def summarize(p):
        def body(i, _):
            pair = [SW * i + u for u in range(SW)]
            values = [(short(k_ref, 1, t, u) * short(v_ref, 2, t, u)).astype(bf16) for u, t in enumerate(pair)]
            for u, t in enumerate(pair):
                mixed[t] = values[u]
                sides = jnp.concatenate([values[u][:half], values[u][half:]], axis=1)
                spread = jnp.dot(leaving[tile_at(t), :], sides, preferred_element_type=f32)
                one, two = pick(spread[:, :LANES]), pick(spread[:, LANES:])
                state = jnp.exp2(rate[:, tile_at(t)] * float(half)) * one + two
                first_half[:, tile_at(t)] = one
                total[:, tile_at(t)] = state
                first_out[p, :, tile_at(t - p * part_tiles)] = state.astype(bf16)
            return 0

        lax.fori_loop(p * part_tiles // SW, (p + 1) * part_tiles // SW, body, 0, unroll=SU)

    causal = (lax.broadcasted_iota(jnp.int32, (half, LANES), 1)
              <= lax.broadcasted_iota(jnp.int32, (half, LANES), 0))

    def diagonal(state):
        fine = state.astype(bf16).astype(f32)
        return jnp.concatenate([jnp.where(lane_group == j, fine, 0.0) for j in range(per)], axis=0).astype(bf16)

    def convolve_tile(i, slot):
        values = mixed[i]
        first, second = values[:half], values[half:]
        sides = jnp.concatenate([first, second], axis=1)
        ent = entering[i]
        lines = hrev[pl.ds(pl.multiple_of(i * per, per), per), :]
        left_side, right_side = [], []
        both_groups = jnp.concatenate([lane_group, lane_group], axis=1)
        for j in range(per):
            line = jnp.broadcast_to(lines[j:j + 1], (half, LANES))
            block = pltpu.roll(line, 1, 1, stride=1, stride_axis=0)
            left_side.append(jnp.where(causal, block, 0.0).astype(bf16))
            right_side.append(jnp.where(both_groups == j, sides, jnp.zeros_like(sides)))
        state = diagonal(first_half[:, tile_at(i)] * wide_weight[:, tile_at(i)])
        product = jnp.dot(jnp.concatenate(left_side, axis=1), jnp.concatenate(right_side, axis=0),
                          preferred_element_type=f32)
        inner = jnp.dot(ent, state, preferred_element_type=f32)
        skip = skip_ref[:, tile_at(i)]
        conv[:half, tile_at(i)] = product[:, :LANES] + skip * first.astype(f32)
        conv[half:, tile_at(i)] = product[:, LANES:] + inner + skip * second.astype(f32)
        q_short[i] = short(q_ref, 0, i, slot).astype(bf16)

    def convolve(i, _):
        for u in range(CW):
            convolve_tile(CW * i + u, u)
        return 0

    carry[...] = jnp.zeros_like(carry)
    core = lax.rem(me, 2)

    def arrive(p, r):
        bit = 1 << r
        last = r == rounds - 1
        upper = lax.rem(lax.div(me, bit), 2) == 1
        block_rate = float(tok * bit)
        offset = ((lax.rem(me, bit) - core) * tok).astype(f32) if r else None

        def merge(i, _):
            local = core * half_tiles + i
            place = tile_at(p * part_tiles + local)
            theirs = (state_in[p, r, :, tile_at(i)] if r else first_in[p, :, tile_at(local)]).astype(f32)
            logs = rate[:, place]
            if r:
                inward = jnp.exp2(logs * offset) * theirs
                carry[p, :, tile_at(i)] += jnp.where(upper, inward, 0.0)
            if not last:
                mine = total[:, place]
                later = jnp.where(upper, mine, theirs)
                before = jnp.where(upper, theirs, mine)
                both = jnp.exp2(logs * block_rate) * before + later
                total[:, place] = both
                state_out[p, r + 1, :, tile_at(i)] = both.astype(bf16)
            return 0

        def receive():
            scan_copy(p, r).wait_recv()
            lax.fori_loop(0, half_tiles, merge, 0, unroll=4)

        if last:
            pl.when(upper)(receive)
            share_copy(p).start()
        else:
            receive()
            following = scan_copy(p, r + 1)
            if r + 1 == rounds - 1:
                pl.when(lax.rem(lax.div(me, 2 * bit), 2) == 0)(following.start)
            else:
                following.start()

    for p in range(PARTS):
        summarize(p)
        scan_copy(p, 0).start()
        if p:
            arrive(p - 1, 0)

    loads[6].wait()
    events = [(PARTS - 1, 0)] + [(p, r) for r in range(1, rounds) for p in range(PARTS)]
    shares = [LEAD] + [FIRST if p == 0 else THEN for r in range(1, rounds) for p in range(PARTS)]
    steps = tiles // CW
    done = 0
    for k, (p, r) in enumerate(events):
        end = (steps * sum(shares[:k + 1]) + sum(shares) // 2) // sum(shares)
        if end > done:
            lax.fori_loop(done, end, convolve, 0, unroll=CU)
        done = end
        arrive(p, r)

    def assemble(p):
        def body(i, _):
            for part, side in ((carry, core), (carry_in, 1 - core)):
                local = side * half_tiles + i
                place = tile_at(p * part_tiles + local)
                entry = part[p, :, tile_at(i)]
                moved = jnp.exp2(rate[:, place] * float(tok)) * entry + first_in[p, :, tile_at(local)].astype(f32)
                total[:, place] = jnp.where(core == 1, moved, entry)
            return 0

        lax.fori_loop(0, half_tiles, body, 0, unroll=2)

    square[...] = jnp.zeros_like(square)

    def gated_tile(i):
        state = total[:, tile_at(i)] * wide_weight[:, tile_at(i)]
        later = state * jnp.exp2(rate[:, tile_at(i)] * float(half))
        columns = [diagonal(state), diagonal(later)]
        ent = entering[i]
        carried = jnp.dot(ent, jnp.concatenate(columns, axis=1),
                          preferred_element_type=f32)
        gated = []
        for side in range(2):
            rows = slice(side * half, (side + 1) * half)
            g = q_short[i, rows, :].astype(f32) * (conv[rows, tile_at(i)] + carried[:, side * LANES:(side + 1) * LANES])
            conv[rows, tile_at(i)] = g
            gated.append(g)
        return gated

    def gate(i, _):
        done = [gated_tile(GW * i + u) for u in range(GW)]
        for side in range(2):
            rows = slice(side * half, (side + 1) * half)
            square[rows, :] += sum(g[side] * g[side] for g in done)
        return 0

    for p in range(PARTS):
        share_copy(p).wait()
        assemble(p)
        lax.fori_loop(p * part_tiles // GW, (p + 1) * part_tiles // GW, gate, 0, unroll=GU)

    sums = jnp.sum(square[...].T, axis=0, keepdims=True)
    square_out[...] = jnp.broadcast_to(sums, square_out.shape)
    copies = []
    for d in range(1, nch):
        c = pltpu.make_async_remote_copy(square_out, square_in.at[d - 1], square_send.at[d - 1], square_recv.at[d - 1],
                                         device_id={"ch": lax.rem(mych + d, nch)}, device_id_type=MESH)
        c.start()
        copies.append(c)
    for d, c in enumerate(copies):
        c.wait()
        sums = sums + square_in[d, 0:1, :]
    scale = lax.rsqrt(sums / (channels * nch) + 1e-5)
    square[...] = jnp.broadcast_to(scale, (LANES, tok)).T

    @pl.when(me < n - 1)
    def _():
        halo.wait_send()

    for p in range(PARTS):
        for r in range(rounds):
            bit = 1 << r
            copy = scan_copy(p, r)
            if r == rounds - 1:
                @pl.when(lax.rem(lax.div(me, bit), 2) == 0)
                def _():
                    copy.wait_send()
            else:
                copy.wait_send()


def normalize(gated_ref, scale_ref, gain_ref, out_hbm, out_ref, sem):
    pieces = out_ref.shape[0]
    width = out_ref.shape[2]

    def copy(j):
        return pltpu.make_async_copy(out_ref.at[j], out_hbm.at[:, j * width:(j + 1) * width], sem.at[j])

    for j in range(pieces):
        for i in range(width // LANES):
            place = slice(j * width + i * LANES, j * width + (i + 1) * LANES)
            out_ref[j, :, i * LANES:(i + 1) * LANES] = (gated_ref[:, place] * scale_ref[...] * gain_ref[:, place]).astype(bf16)
        copy(j).start()
    for j in range(pieces):
        copy(j).wait()


def on_device(n, nch, q_proj, k_proj, v_proj, short_filter, log_decay, residue, skip_bias, norm_gain):
    tok, channels = q_proj.shape
    groups, modes = log_decay.shape
    rounds = n.bit_length() - 1
    assert channels % (4 * LANES) == 0 and n == 1 << rounds and rounds > 1 and channels == groups * modes
    vmem = pl.BlockSpec(memory_space=pltpu.VMEM)
    dma = pltpu.SemaphoreType.DMA
    PARTS = min(MOST_PARTS, channels // (4 * LANES))
    part = channels // PARTS
    gated, scale = pl.pallas_call(
        functools.partial(kernel, n, nch, rounds, modes),
        out_shape=(jax.ShapeDtypeStruct((tok, channels), f32), jax.ShapeDtypeStruct((tok, LANES), f32)),
        in_specs=[pl.BlockSpec(memory_space=pltpu.HBM)] * 7,
        out_specs=(vmem, vmem),
        scratch_shapes=[
            pltpu.VMEM((tok, channels), bf16),
            pltpu.VMEM((tok, channels), bf16),
            pltpu.VMEM((tok, channels), bf16),
            pltpu.VMEM((9, channels), f32),
            pltpu.VMEM((modes, groups), f32),
            pltpu.VMEM((modes, groups), f32),
            pltpu.VMEM((1, channels), f32),
            pltpu.VMEM((3, 16, channels), bf16),
            pltpu.VMEM((8, channels), bf16),
            pltpu.VMEM((8, channels), bf16),
            pltpu.VMEM((3 * max(SW, CW), tok + 8, LANES), f32),
            pltpu.VMEM((channels, tok // 2), bf16),
            pltpu.VMEM((groups, tok // 2), f32),
            pltpu.VMEM((channels // LANES, tok // 2, LANES), bf16),
            pltpu.VMEM((channels // LANES, tok, LANES), bf16),
            pltpu.VMEM((channels // LANES, tok, LANES), bf16),
            pltpu.VMEM((modes, channels), f32),
            pltpu.VMEM((modes, channels), f32),
            pltpu.VMEM((modes, channels), f32),
            pltpu.VMEM((modes, channels), f32),
            pltpu.VMEM((PARTS, modes, part // 2), f32),
            pltpu.VMEM((PARTS, modes, part // 2), f32),
            pltpu.VMEM((PARTS, modes, part), bf16),
            pltpu.VMEM((PARTS, modes, part), bf16),
            pltpu.VMEM((PARTS, rounds, modes, part // 2), bf16),
            pltpu.VMEM((PARTS, rounds, modes, part // 2), bf16),
            pltpu.VMEM((8, tok), f32),
            pltpu.VMEM((max(nch - 1, 1), 8, tok), f32),
            dma, dma, dma((PARTS, rounds)), dma((PARTS, rounds)), dma((max(nch - 1, 1),)), dma((max(nch - 1, 1),)),
            dma((7,)), dma((3,)), dma((PARTS,)), dma((PARTS,)),
        ],
        compiler_params=pltpu.CompilerParams(collective_id=0, has_side_effects=True,
                                             vmem_limit_bytes=LIMIT_A),
    )(*[pltpu.with_memory_space_constraint(x, pltpu.HBM) for x in (q_proj, k_proj, v_proj, short_filter, log_decay.T, residue.T, skip_bias.reshape(1, channels))])
    pieces = 8
    return pl.pallas_call(
        normalize,
        out_shape=jax.ShapeDtypeStruct((tok, channels), bf16),
        in_specs=[vmem, vmem, vmem],
        out_specs=pl.BlockSpec(memory_space=pltpu.HBM),
        scratch_shapes=[pltpu.VMEM((pieces, tok, channels // pieces), bf16), dma((pieces,))],
        compiler_params=pltpu.CompilerParams(vmem_limit_bytes=LIMIT_B),
    )(gated, scale, norm_gain.reshape(1, channels))


UP = 8
SW, SU, CW, CU, GW, GU, LEAD, FIRST, THEN = 2, 4, 2, 2, 2, 4, 2, 6, 1
LIMIT_A = 28 * 1024 * 1024
LIMIT_B = 16 * 1024 * 1024


def solution(mesh):
    return jax.shard_map(
        functools.partial(on_device, mesh.shape["seq"], mesh.shape["ch"]),
        mesh=mesh,
        in_specs=(P("seq", "ch"), P("seq", "ch"), P("seq", "ch"), P(None, "ch"),
                  P("ch", None), P("ch", None), P("ch"), P("ch")),
        out_specs=P("seq", "ch"),
        check_vma=False,
    )
```
